128 devices in a mesh: expert: 8 (over z, core), shard: 16 (over y, x).
Axes of the slice: x: 4, y: 4, z: 4, core: 2. Of those that a mesh axis runs over, the one named last changes fastest.
Arguments:
- tokens: bfloat16 [16384, 896], P(('expert', 'shard')), may hold values from -6 to 6
- routes: int32 [16384, 2], P(('expert', 'shard')), may hold values from 0 to 7, all different within a row; in each aligned block of 128 rows (0 to 127, 128 to 255, ...) at most 48 rows name the same one
- gate_num: int32 [16384, 2], P(('expert', 'shard')), may hold values from 1 to 15
- student_gate: bfloat16 [8, 896, 4864], P('expert', None, 'shard'), may hold values from -0.1875 to 0.1875
- student_up: bfloat16 [8, 896, 4864], P('expert', None, 'shard'), may hold values from -0.1875 to 0.1875
- student_down: bfloat16 [8, 4864, 896], P('expert', 'shard'), may hold values from -0.078125 to 0.078125
- teacher_gate: bfloat16 [8, 896, 4864], P('expert', None, 'shard'), may hold values from -0.1875 to 0.1875
- teacher_up: bfloat16 [8, 896, 4864], P('expert', None, 'shard'), may hold values from -0.1875 to 0.1875
- teacher_down: bfloat16 [8, 4864, 896], P('expert', 'shard'), may hold values from -0.078125 to 0.078125
Outputs:
- residual: bfloat16 [16384, 896], P(('expert', 'shard'))
The draws below stay inside these ranges and needn't reach their ends.
Inputs may be any that keep to these rules, and one draw needn't show every extreme that they name: `routes`: each row names two different experts. Among the rows of one device no expert is named by more than 48 rows, and in every draw some expert is named by exactly 48 rows of some device.
All inputs are finite; a program needn't handle non-finite values.
Results may differ from the reference program's by a relative error of at most 0.0049.
Values may be sent and summed in bfloat16 or wider, within the bound.
No kernel may reach another device: no remote copies, remote signals or barrier semaphores. Data moves between devices by JAX's collectives and lax.ppermute only.
A program may use at most 128 MiB of HBM per device.

```python
import math
import jax
import jax.numpy as jnp
import numpy as np

D = 896
FF = 4864
TOK_DEV = 128
EXPERTS = 8
CAP = 48
TOKENS = 16384
DEVICES = 128


def plant(entries, own_key, smallest, top_value):
    longest = entries.shape.index(max(entries.shape))
    spots = []
    for shift in (0, 1):
        where = [jax.random.randint(jax.random.fold_in(own_key, axis), (), 0, length) for axis, length in enumerate(entries.shape)]
        where[longest] = (where[longest] + shift) % entries.shape[longest]
        spots.append(tuple(where))
    return entries.at[spots[0]].set(smallest).at[spots[1]].set(top_value)


def block_scale(stream_key, dims, split, low, largest):
    def one(axis_at, shards_of):
        heights = jax.random.uniform(jax.random.fold_in(jax.random.fold_in(stream_key, 6), axis_at), (shards_of,), jnp.float32, low / len(split), largest / len(split))
        return jnp.repeat(jnp.exp(heights), dims[axis_at] // shards_of).reshape((-1,) + (1,) * (len(dims) - axis_at - 1))

    level = one(*split[0])
    for cut in split[1:]:
        level = level * one(*cut)
    return level


def deal_out(stream_key, own, number, rows, count, top, limit, slope):
    order = jax.random.permutation(stream_key, count)
    crowded, usual = shares(count, rows * top, limit, slope, True), shares(count, rows * top, limit, slope, False)
    places = jnp.arange(count)

    def named(sizes, turn):
        used = int((sizes > 0).sum())
        fixed = max(1, used // 4)
        passed = fixed + (places - fixed + turn * (used - fixed)) % max(1, count - fixed)
        return jnp.zeros((count,), jnp.int32).at[order[jnp.where(places < fixed, places, passed)]].set(jnp.asarray(sizes, jnp.int32))

    sizes = jnp.where(number % 4 == 0, named(crowded, number // 4), named(usual, number - number // 4 - 1))
    mixed = jax.random.permutation(jax.random.fold_in(own, 3), count)
    donor, sink = mixed[0:count // 2 * 2:2], mixed[1:count // 2 * 2:2]
    room = jnp.minimum(sizes[donor] - 1, limit - sizes[sink]) // 2
    room = jnp.where((donor == order[0]) | (sink == order[0]) | (sizes[sink] == 0), 0, jnp.maximum(room, 0))
    passed = jax.random.randint(jax.random.fold_in(own, 4), (count // 2,), 0, 1 << 20) % (room + 1)
    sizes = sizes.at[donor].add(-passed).at[sink].add(passed)
    members = jnp.searchsorted(jnp.cumsum(sizes), jnp.arange(rows * top), side="right").astype(jnp.int32)
    table = members.reshape(top, rows).T
    table = table[jax.random.permutation(jax.random.fold_in(own, 1), rows)]
    turn = jax.random.randint(jax.random.fold_in(own, 2), (rows, 1), 0, top)
    return jnp.take_along_axis(table, (jnp.arange(top)[None, :] + turn) % top, axis=1)


def shares(amount, total, bound, slope, full):
    weights = [(1 << 20) // math.isqrt(rank ** slope) + 1 for rank in range(1, amount + 1)]
    largest = bound if full else min(bound, max(-(-total // amount), total * weights[0] // sum(weights)))
    least = 1 if total - largest >= amount - 1 else 0
    given, surplus = [largest] + [least] * (amount - 1), total - largest - least * (amount - 1)
    while surplus > 0:
        free = [i for i in range(1, amount) if given[i] < largest] or [i for i in range(1, amount) if given[i] < bound]
        pool, remaining = sum([weights[i] for i in free]), surplus
        for i in free:
            more = min(bound - given[i], max(1, remaining * weights[i] // pool), surplus)
            given[i] = given[i] + more
            surplus = surplus - more
    return np.array(given)


def centred(key, shape, deviation, most, shards=(), kind=jnp.bfloat16):
    values = deviation * jax.random.normal(key, shape, jnp.float32)
    if shards:
        values = values * block_scale(key, shape, shards, -0.22, 0.18)
    return jnp.clip(values, -most, most).astype(kind)


def setup_inputs(seed: int = 0) -> dict:
    key_list = jax.random.split(jax.random.key(seed), 10)
    tokens = centred(key_list[0], (TOKENS, D), 1.0, 6.0, ((0, 128),))
    routes_keys = jax.random.split(jax.random.fold_in(key_list[1], 1), TOKENS // TOK_DEV)
    routes_turns = jax.random.permutation(jax.random.fold_in(key_list[1], 3), TOKENS // TOK_DEV)
    routes = jax.vmap(lambda own, number: deal_out(jax.random.fold_in(key_list[1], 2), own, number, TOK_DEV, EXPERTS, 2, CAP, 2))(routes_keys, routes_turns).reshape((TOKENS, 2))
    gate_num = plant(jax.random.randint(key_list[2], (TOKENS, 2), 1, 16), jax.random.fold_in(key_list[2], 1), 1, 15).astype(jnp.int32)
    student_gate = centred(key_list[3], (EXPERTS, D, FF), D ** -0.5, 0.1875, ((0, 8), (2, 16)))
    student_up = centred(key_list[4], (EXPERTS, D, FF), D ** -0.5, 0.1875, ((0, 8), (2, 16)))
    student_down = centred(key_list[5], (EXPERTS, FF, D), FF ** -0.5, 0.078125, ((0, 8), (1, 16)))
    teacher_gate = centred(key_list[6], (EXPERTS, D, FF), D ** -0.5, 0.1875, ((0, 8), (2, 16)))
    teacher_up = centred(key_list[7], (EXPERTS, D, FF), D ** -0.5, 0.1875, ((0, 8), (2, 16)))
    teacher_down = centred(key_list[8], (EXPERTS, FF, D), FF ** -0.5, 0.078125, ((0, 8), (1, 16)))
    return {"tokens": tokens, "routes": routes, "gate_num": gate_num, "student_gate": student_gate, "student_up": student_up, "student_down": student_down, "teacher_gate": teacher_gate, "teacher_up": teacher_up, "teacher_down": teacher_down}


def slot_targets(route_block):
    flat_ids = route_block.reshape(-1)
    onehot = (flat_ids[:, None] == jnp.arange(EXPERTS, dtype=jnp.int32)[None, :]).astype(jnp.int32)
    earlier = jnp.cumsum(onehot, axis=0) - onehot
    slot = jnp.sum(earlier * onehot, axis=1)
    return (flat_ids * CAP + slot).astype(jnp.int32)


def buffer_of(token_block, target):
    tok_rows = token_block.shape[0]
    source_row = jnp.full((EXPERTS * CAP,), tok_rows, jnp.int32)
    source_row = source_row.at[target].set(jnp.arange(tok_rows * 2, dtype=jnp.int32) // 2)
    padded = jnp.concatenate([token_block, jnp.zeros((1, D), jnp.bfloat16)], axis=0)
    return padded[source_row].reshape(EXPERTS, CAP, D)


def half_net(row_block, gate_proj, up_proj, down_proj):
    gate_val = jnp.dot(row_block, gate_proj, preferred_element_type=jnp.float32)
    up_val = jnp.dot(row_block, up_proj, preferred_element_type=jnp.float32)
    hidden = (jax.nn.silu(gate_val) * up_val).astype(jnp.bfloat16)
    return jnp.dot(hidden, down_proj, preferred_element_type=jnp.float32)


def reference(tokens, routes, gate_num, student_gate, student_up, student_down, teacher_gate, teacher_up, teacher_down):
    blocks = tokens.reshape(DEVICES, TOK_DEV, D)
    targets = jax.vmap(slot_targets)(routes.reshape(DEVICES, TOK_DEV, 2))
    buffers = jax.vmap(buffer_of)(blocks, targets)
    numerators = gate_num.astype(jnp.float32)
    gate_share = (numerators / jnp.sum(numerators, axis=1, keepdims=True)).reshape(DEVICES, TOK_DEV * 2)
    slots = targets % CAP
    owners = targets // CAP
    accumulated = jnp.zeros((DEVICES, TOK_DEV, D), jnp.float32)
    for expert_id in range(EXPERTS):
        row_block = buffers[:, expert_id].reshape(DEVICES * CAP, D)
        expert_diff = half_net(row_block, student_gate[expert_id], student_up[expert_id], student_down[expert_id]) - half_net(row_block, teacher_gate[expert_id], teacher_up[expert_id], teacher_down[expert_id])
        expert_diff = expert_diff.reshape(DEVICES, CAP, D)
        picked = jnp.take_along_axis(expert_diff, slots[:, :, None], axis=1)
        weight = jnp.where(owners == expert_id, gate_share, jnp.float32(0.0))
        contrib = (weight[:, :, None] * picked).reshape(DEVICES, TOK_DEV, 2, D)
        accumulated = accumulated + jnp.sum(contrib, axis=2)
    return accumulated.reshape(TOKENS, D).astype(jnp.bfloat16)
```

```python
import functools

import jax
import jax.numpy as jnp
from jax import lax
from jax.experimental import pallas as pl
from jax.experimental.pallas import tpu as pltpu
from jax.sharding import PartitionSpec as P

AXES = ("expert", "shard")
BF16 = jnp.bfloat16
F32 = jnp.float32
LANES = 128
CAP = 48
EXPERTS = 8
VMEM_LIMIT = 56 * 1024 * 1024


def dev(z, c, y, x):
    return ((z % 4 * 2 + c % 2) * 4 + y % 4) * 4 + x % 4


COORDS = [(z, c, y, x) for z in range(4) for c in range(2) for y in range(4) for x in range(4)]


def ring(step, weights):
    return [
        (dev(z, c, y, x), dev(z, c, y, x + step) if (c == 0) == weights else dev(z, c, y + step, x))
        for z, c, y, x in COORDS
    ]


def hop(offset, back=False):
    dz, dc = offset // 2, offset % 2
    pairs = [(dev(z, c, y, x), dev(z + dz, c + dc, y, x)) for z, c, y, x in COORDS]
    return [(b, a) for a, b in pairs] if back else pairs


def send(value, pairs):
    return lax.ppermute(value, AXES, pairs)


def whole(count):
    return [pl.BlockSpec(memory_space=pltpu.VMEM)] * count


def pack_kernel(teacher, gate_ref, up_ref, down_ref, out_ref):
    width, units = gate_ref.shape
    full = units // LANES
    tail = units % LANES
    for n in range(full):
        out_ref[2 * n * width : (2 * n + 1) * width] = gate_ref[:, n * LANES : (n + 1) * LANES]
        out_ref[(2 * n + 1) * width : (2 * n + 2) * width] = up_ref[:, n * LANES : (n + 1) * LANES]
    gate_tail = gate_ref[:, full * LANES :]
    up_tail = up_ref[:, full * LANES :]
    zeros = functools.partial(jnp.zeros, dtype=BF16)
    gap = LANES // 2 - tail
    if teacher:
        wrap = LANES // 2 - tail
        pieces = [
            up_tail[:, wrap:],
            zeros((width, tail - (tail - wrap))),
            gate_tail,
            zeros((width, LANES // 2 - tail)),
            up_tail[:, :wrap],
        ]
    else:
        pieces = [gate_tail, zeros((width, gap)), up_tail, zeros((width, gap))]
    out_ref[2 * full * width : (2 * full + 1) * width] = jnp.concatenate(pieces, axis=1)
    base = (2 * full + 1) * width
    for m in range(width // LANES):
        block = down_ref[:, m * LANES : (m + 1) * LANES]
        out_ref[base + m * units : base + (m + 1) * units] = -block if teacher else block


def pack(gate, up, down, teacher):
    width, units = gate.shape
    rows = (2 * (units // LANES) + 1) * width + width // LANES * units
    return pl.pallas_call(
        functools.partial(pack_kernel, teacher),
        out_shape=jax.ShapeDtypeStruct((rows, LANES), BF16),
        in_specs=whole(3),
        out_specs=pl.BlockSpec(memory_space=pltpu.VMEM),
        compiler_params=pltpu.CompilerParams(vmem_limit_bytes=VMEM_LIMIT),
        cost_estimate=pl.CostEstimate(flops=0, bytes_accessed=7_000_000, transcendentals=0),
        name="pack_weights",
    )(gate, up, down)


def places(here_ref, routes_ref):
    here = here_ref[0]
    tokens = routes_ref.shape[0]
    first, second = routes_ref[:, 0:1], routes_ref[:, 1:2]
    lane = lax.broadcasted_iota(jnp.int32, (tokens, LANES), 1)
    named = ((lane == first).astype(F32) + (lane == second).astype(F32)).astype(BF16)
    row = lax.broadcasted_iota(jnp.int32, (tokens, tokens), 0)
    col = lax.broadcasted_iota(jnp.int32, (tokens, tokens), 1)
    earlier = jnp.dot((col < row).astype(F32).astype(BF16), named, preferred_element_type=F32)
    found = []
    for ids, extra in ((first, 0), (second, (first == second).astype(jnp.int32))):
        slot = jnp.sum(jnp.where(lane == ids, earlier, 0.0), axis=1, keepdims=True).astype(jnp.int32) + extra
        offset = (((ids >> 1) - (here >> 1)) & 3) * 2 + ((ids - here) & 1)
        found.append(offset * CAP + slot)
    return found


def dispatch_kernel(here_ref, routes_ref, tokens_ref, *out_refs):
    first, second = places(here_ref, routes_ref)
    tokens = tokens_ref.shape[0]
    slots = lax.broadcasted_iota(jnp.int32, (tokens, EXPERTS * CAP), 1)
    chosen = ((slots == first) | (slots == second)).astype(F32).astype(BF16)
    rows = lax.dot_general(chosen, tokens_ref[...], (((0,), (0,)), ((), ())), preferred_element_type=F32).astype(BF16)
    for i, out_ref in enumerate(out_refs):
        out_ref[...] = rows[i * CAP : (i + 1) * CAP]


def dispatch(here, routes, tokens):
    width = tokens.shape[1]
    return pl.pallas_call(
        dispatch_kernel,
        out_shape=[jax.ShapeDtypeStruct((CAP, width), BF16)] * EXPERTS,
        in_specs=[pl.BlockSpec(memory_space=pltpu.SMEM)] + whole(2),
        out_specs=whole(EXPERTS),
        compiler_params=pltpu.CompilerParams(vmem_limit_bytes=VMEM_LIMIT),
        cost_estimate=pl.CostEstimate(flops=100_000_000, bytes_accessed=1_000_000, transcendentals=0),
        name="dispatch_rows",
    )(here, routes, tokens)


def combine_kernel(here_ref, routes_ref, gates_ref, *refs):
    *block_refs, out_ref = refs
    first, second = places(here_ref, routes_ref)
    tokens = routes_ref.shape[0]
    gates = gates_ref[...].astype(F32)
    share = gates / jnp.sum(gates, axis=1, keepdims=True)
    slots = lax.broadcasted_iota(jnp.int32, (tokens, EXPERTS * CAP), 1)
    weight = jnp.where(slots == first, share[:, 0:1], 0.0) + jnp.where(slots == second, share[:, 1:2], 0.0)
    rows = jnp.concatenate([r[...] for r in block_refs], axis=0)
    total = None
    for _ in range(3):
        part = weight.astype(BF16)
        weight = weight - part.astype(F32)
        term = jnp.dot(part, rows, preferred_element_type=F32)
        total = term if total is None else total + term
    out_ref[...] = total.astype(BF16)


def combine(here, routes, gates, blocks):
    tokens, width = routes.shape[0], blocks[0].shape[1]
    return pl.pallas_call(
        combine_kernel,
        out_shape=jax.ShapeDtypeStruct((tokens, width), BF16),
        in_specs=[pl.BlockSpec(memory_space=pltpu.SMEM)] + whole(2 + EXPERTS),
        out_specs=pl.BlockSpec(memory_space=pltpu.VMEM),
        compiler_params=pltpu.CompilerParams(vmem_limit_bytes=VMEM_LIMIT),
        cost_estimate=pl.CostEstimate(flops=300_000_000, bytes_accessed=1_000_000, transcendentals=0),
        name="combine_rows",
    )(here, routes, gates, *blocks)


def net_kernel(n_x, n_shards, acc_at, rows_of, units, *refs):
    x_refs, refs = refs[:n_x], refs[n_x:]
    piece_refs, refs = refs[: 2 * n_shards], refs[2 * n_shards :]
    if acc_at is not None:
        acc_in, refs = refs[0], refs[1:]
    n_out = len(rows_of)
    out_refs, refs = refs[:n_out], refs[n_out:]
    x, gate_up, down, total, x_sem, w_sem, acc_sem = refs
    rows, width = x.shape
    full = units // LANES
    main, tail = full * LANES, units % LANES
    side = (2 * full + 1) * LANES
    blocks = 2 * full + 1

    def shard_copies(s):
        copies = []
        for half in range(2):
            piece = piece_refs[2 * s + half]
            for n in range(blocks):
                copies.append((piece.at[pl.ds(n * width, width)], gate_up.at[s, :, pl.ds(half * side + n * LANES, LANES)]))
            for m in range(width // LANES):
                at = blocks * width + m * units
                lanes = pl.ds(m * LANES, LANES)
                copies.append((piece.at[pl.ds(at, main)], down.at[s, pl.ds(half * main, main), lanes]))
                copies.append((piece.at[pl.ds(at + main, tail)], down.at[s, pl.ds(2 * main + half * tail, tail), lanes]))
        return [pltpu.make_async_copy(a, b, w_sem.at[s, i]) for i, (a, b) in enumerate(copies)]

    x_copies, at = [], 0
    for i, ref in enumerate(x_refs):
        x_copies.append(pltpu.make_async_copy(ref, x.at[pl.ds(at, ref.shape[0])], x_sem.at[i]))
        at += ref.shape[0]
    for copy in x_copies:
        copy.start()
    for copy in shard_copies(0):
        copy.start()
    if acc_at is not None:
        acc_copy = pltpu.make_async_copy(acc_in.at[pl.ds(acc_at, rows)], total, acc_sem)
        acc_copy.start()
    for s in range(1, n_shards):
        for copy in shard_copies(s):
            copy.start()
    for s in range(n_shards):
        down[s, 2 * main + 2 * tail :, :] = jnp.zeros((down.shape[1] - 2 * main - 2 * tail, width), BF16)
    for copy in x_copies:
        copy.wait()

    tile = 384
    lane = lax.broadcasted_iota(jnp.int32, (tile, LANES), 1)

    def silu(v):
        return v / (1.0 + jnp.exp(-v))

    for s in range(n_shards):
        for copy in shard_copies(s):
            copy.wait()
        if s == 0 and acc_at is not None:
            acc_copy.wait()

        @pl.loop(0, rows // tile)
        def _(r):
            at = pl.ds(pl.multiple_of(r * tile, tile), tile)
            wide = jnp.dot(x[at, :], gate_up[s], preferred_element_type=F32)
            hidden, tails = [], []
            for half in range(2):
                for n in range(full):
                    lo = half * side + 2 * n * LANES
                    hidden.append((silu(wide[:, lo : lo + LANES]) * wide[:, lo + LANES : lo + 2 * LANES]).astype(BF16))
                lo = half * side + 2 * full * LANES
                last = wide[:, lo : lo + LANES]
                tails.append(silu(last) * pltpu.roll(last, LANES // 2, 1))
            both = jnp.where(lane < tail, tails[0], jnp.where(lane < 2 * tail, tails[1], 0.0))
            hidden.append(both.astype(BF16))
            term = jnp.dot(jnp.concatenate(hidden, axis=1), down[s], preferred_element_type=F32)
            if s == 0 and acc_at is None:
                total[at, :] = term
            else:
                total[at, :] += term

    at = 0
    for out_ref, n in zip(out_refs, rows_of):
        out_ref[...] = total[at : at + n].astype(out_ref.dtype)
        at += n


def net(xs, shards, outs, units, acc=None, acc_at=None):
    rows, width = sum(a.shape[0] for a in xs), xs[0].shape[1]
    n = len(shards)
    main_units = units // LANES * LANES
    lanes = 2 * (2 * (units // LANES) + 1) * LANES
    depth = 2 * main_units + LANES
    copies = 2 * (2 * (units // LANES) + 1 + 2 * (width // LANES))
    operands = list(xs) + [p for s in shards for p in s] + ([] if acc is None else [acc])
    return pl.pallas_call(
        functools.partial(net_kernel, len(xs), n, acc_at, tuple(r for r, _ in outs), units),
        out_shape=[jax.ShapeDtypeStruct((r, width), d) for r, d in outs],
        in_specs=[pl.BlockSpec(memory_space=pl.ANY)] * len(operands),
        out_specs=whole(len(outs)),
        scratch_shapes=[
            pltpu.VMEM((rows, width), BF16),
            pltpu.VMEM((n, width, lanes), BF16),
            pltpu.VMEM((n, depth, width), BF16),
            pltpu.VMEM((rows, width), F32),
            pltpu.SemaphoreType.DMA((len(xs),)),
            pltpu.SemaphoreType.DMA((n, copies)),
            pltpu.SemaphoreType.DMA,
        ],
        compiler_params=pltpu.CompilerParams(vmem_limit_bytes=VMEM_LIMIT),
        cost_estimate=pl.CostEstimate(
            flops=rows * width * units * 2 * n * 6,
            bytes_accessed=rows * width * 8 + n * 3_400_000,
            transcendentals=rows * units * 2 * n,
        ),
        name="networks",
    )(*operands)


def per_device(tokens, routes, gate_num, student_gate, student_up, student_down, teacher_gate, teacher_up, teacher_down):
    here = lax.axis_index("expert").astype(jnp.int32).reshape(1)
    units = student_gate.shape[2]
    block = EXPERTS * CAP
    half = block // 2

    student = pack(student_gate[0], student_up[0], student_down[0], False)
    teacher = pack(teacher_gate[0], teacher_up[0], teacher_down[0], True)
    student_next = send(student, ring(1, True))
    teacher_prev = send(teacher, ring(-1, True))
    teacher_next = send(teacher, ring(1, True))
    student_prev = send(student, ring(-1, True))

    out_blocks = dispatch(here, routes, tokens)
    rows = jnp.concatenate([out_blocks[0]] + [send(out_blocks[d], hop(d)) for d in range(1, EXPERTS)], axis=0)
    rows_from_prev = send(rows, ring(1, False))
    rows_from_next = send(rows, ring(-1, False))
    far_a = send(rows_from_prev[:half], ring(1, False))
    far_b = send(rows_from_next[half:], ring(-1, False))

    student_far = send(student_next, ring(1, True))
    teacher_far = send(teacher_prev, ring(-1, True))

    width = tokens.shape[1]
    near = [(student, teacher), (student_next, teacher_next), (student_prev, teacher_prev)]
    far = [(student_far, teacher_far)]
    (partial,) = net([far_a, far_b, rows_from_next, rows_from_prev, rows], near, [(4 * block, F32)], units)
    far_out_a, far_out_b = net([far_a, far_b], far, [(half, BF16), (half, BF16)], units, partial, 0)
    sum_a = send(far_out_a, ring(1, False))
    sum_b = send(far_out_b, ring(-1, False))
    to_next, to_prev, own = net(
        [rows_from_next, rows_from_prev, rows], far, [(block, F32), (block, F32), (block, F32)], units, partial, block
    )
    to_next = jnp.concatenate([to_next[:half] + sum_a.astype(F32), to_next[half:]], axis=0).astype(BF16)
    to_prev = jnp.concatenate([to_prev[:half], to_prev[half:] + sum_b.astype(F32)], axis=0).astype(BF16)
    got_a = send(to_next, ring(1, False))
    got_b = send(to_prev, ring(-1, False))
    mine = (own + got_a.astype(F32) + got_b.astype(F32)).astype(BF16)
    back = [mine[:CAP]] + [send(mine[d * CAP : (d + 1) * CAP], hop(d, True)) for d in range(1, EXPERTS)]
    return combine(here, routes, gate_num, back)


def solution(mesh):
    in_specs = (
        P(("expert", "shard"), None),
        P(("expert", "shard"), None),
        P(("expert", "shard"), None),
        P("expert", None, "shard"),
        P("expert", None, "shard"),
        P("expert", "shard", None),
        P("expert", None, "shard"),
        P("expert", None, "shard"),
        P("expert", "shard", None),
    )
    out_specs = P(("expert", "shard"), None)
    return jax.shard_map(
        per_device, mesh=mesh, in_specs=in_specs, out_specs=out_specs, check_vma=False
    )
```

```python
import functools

import jax
import jax.numpy as jnp
from jax import lax
from jax.experimental import pallas as pl
from jax.experimental.pallas import tpu as pltpu
from jax.sharding import PartitionSpec as P

AXES = ("expert", "shard")
BF16 = jnp.bfloat16
F32 = jnp.float32
CAP = 48
EXPERTS = 8
VMEM_LIMIT = 62 * 1024 * 1024


def dev(z, c, y, x):
    return ((z % 4 * 2 + c % 2) * 4 + y % 4) * 4 + x % 4


COORDS = [(z, c, y, x) for z in range(4) for c in range(2) for y in range(4) for x in range(4)]


def ring(step, weights):
    return [
        (dev(z, c, y, x), dev(z, c, y, x + step) if (c == 0) == weights else dev(z, c, y + step, x))
        for z, c, y, x in COORDS
    ]


def hop(offset, back=False):
    dz, dc = offset // 2, offset % 2
    pairs = [(dev(z, c, y, x), dev(z + dz, c + dc, y, x)) for z, c, y, x in COORDS]
    return [(b, a) for a, b in pairs] if back else pairs


def send(value, pairs):
    return lax.ppermute(value, AXES, pairs)


def barrier(*values):
    return lax.optimization_barrier(values)


def whole(count, space=pltpu.VMEM):
    return [pl.BlockSpec(memory_space=space)] * count


def params():
    return pltpu.CompilerParams(vmem_limit_bytes=VMEM_LIMIT)


def pack_kernel(gate_ref, up_ref, down_ref, out_ref, sems):
    units = gate_ref.shape[0]
    copies = [
        pltpu.make_async_copy(ref, out_ref.at[pl.ds(i * units, units)], sems.at[i])
        for i, ref in enumerate((gate_ref, up_ref, down_ref))
    ]
    for copy in copies:
        copy.start()
    for copy in copies:
        copy.wait()


def pack(gate, up, down):
    units, width = down.shape
    return pl.pallas_call(
        pack_kernel,
        out_shape=jax.ShapeDtypeStruct((3 * units, width), BF16),
        in_specs=whole(3, pltpu.HBM),
        out_specs=pl.BlockSpec(memory_space=pltpu.HBM),
        scratch_shapes=[pltpu.SemaphoreType.DMA((3,))],
        compiler_params=params(),
        cost_estimate=pl.CostEstimate(flops=0, bytes_accessed=3_300_000, transcendentals=0),
        name="pack_weights",
    )(gate.T, up.T, down)


def places(here_ref, routes_ref):
    here = here_ref[0]
    tokens = routes_ref.shape[1]
    first, second = routes_ref[0:1, :], routes_ref[1:2, :]
    expert = lax.broadcasted_iota(jnp.int32, (16, tokens), 0)
    named = ((expert == first).astype(F32) + (expert == second).astype(F32)).astype(BF16)
    before = lax.broadcasted_iota(jnp.int32, (tokens, tokens), 0) < lax.broadcasted_iota(jnp.int32, (tokens, tokens), 1)
    earlier = jnp.dot(named, before.astype(F32).astype(BF16), preferred_element_type=F32)
    found = []
    for ids, extra in ((first, 0), (second, (first == second).astype(jnp.int32))):
        slot = jnp.sum(jnp.where(expert == ids, earlier, 0.0), axis=0, keepdims=True).astype(jnp.int32) + extra
        offset = (((ids >> 1) - (here >> 1)) & 3) * 2 + ((ids - here) & 1)
        found.append(offset * CAP + slot)
    return found


def dispatch_kernel(here_ref, routes_ref, tokens_ref, *out_refs):
    first, second = places(here_ref, routes_ref)
    slots = lax.broadcasted_iota(jnp.int32, (EXPERTS * CAP, tokens_ref.shape[0]), 0)
    chosen = ((slots == first) | (slots == second)).astype(F32).astype(BF16)
    rows = jnp.dot(chosen, tokens_ref[...], preferred_element_type=F32).astype(BF16)
    for i, out_ref in enumerate(out_refs):
        out_ref[...] = rows[i * CAP : (i + 1) * CAP]


def dispatch(here, routes, tokens):
    width = tokens.shape[1]
    return pl.pallas_call(
        dispatch_kernel,
        out_shape=[jax.ShapeDtypeStruct((CAP, width), BF16)] * EXPERTS,
        in_specs=whole(1, pltpu.SMEM) + whole(2),
        out_specs=whole(EXPERTS),
        compiler_params=params(),
        cost_estimate=pl.CostEstimate(flops=100_000_000, bytes_accessed=1_000_000, transcendentals=0),
        name="dispatch_rows",
    )(here, routes, tokens)


def shares_kernel(here_ref, routes_ref, gates_ref, high_ref, low_ref):
    first, second = places(here_ref, routes_ref)
    gates = gates_ref[...].astype(F32)
    share = gates / jnp.sum(gates, axis=0, keepdims=True)
    slots = lax.broadcasted_iota(jnp.int32, (EXPERTS * CAP, routes_ref.shape[1]), 0)
    weight = jnp.where(slots == first, share[0:1], 0.0) + jnp.where(slots == second, share[1:2], 0.0)
    weight = weight.T
    high = weight.astype(BF16)
    high_ref[...] = high
    low_ref[...] = (weight - high.astype(F32)).astype(BF16)


def shares(here, routes, gates):
    tokens = routes.shape[1]
    return pl.pallas_call(
        shares_kernel,
        out_shape=[jax.ShapeDtypeStruct((tokens, EXPERTS * CAP), BF16)] * 2,
        in_specs=whole(1, pltpu.SMEM) + whole(2),
        out_specs=whole(2),
        compiler_params=params(),
        cost_estimate=pl.CostEstimate(flops=10_000_000, bytes_accessed=1_000_000, transcendentals=0),
        name="gate_shares",
    )(here, routes, gates)


def combine_kernel(high_ref, low_ref, *refs):
    *block_refs, out_ref = refs
    rows = jnp.concatenate([r[...] for r in block_refs], axis=0)
    total = jnp.dot(high_ref[...], rows, preferred_element_type=F32)
    total += jnp.dot(low_ref[...], rows, preferred_element_type=F32)
    out_ref[...] = total.astype(BF16)


def combine(high, low, blocks):
    tokens, width = high.shape[0], blocks[0].shape[1]
    return pl.pallas_call(
        combine_kernel,
        out_shape=jax.ShapeDtypeStruct((tokens, width), BF16),
        in_specs=whole(2 + EXPERTS),
        out_specs=pl.BlockSpec(memory_space=pltpu.VMEM),
        compiler_params=params(),
        cost_estimate=pl.CostEstimate(flops=200_000_000, bytes_accessed=1_000_000, transcendentals=0),
        name="combine_rows",
    )(high, low, *blocks)


def net_kernel(n_x, teacher, acc_at, outs, tile, unrolled, *refs):
    n_pieces = len(teacher)
    x_refs, refs = refs[:n_x], refs[n_x:]
    piece_refs, refs = refs[:n_pieces], refs[n_pieces:]
    if acc_at is not None:
        acc_ref, refs = refs[0], refs[1:]
    out_refs, refs = refs[: len(outs)], refs[len(outs) :]
    x, gate_up, down, total, stage, x_sem, w_sem, acc_sem, out_sem = refs
    rows, width = x.shape
    units = piece_refs[0].shape[0] // 3
    n_chunks, depth = down.shape[0], down.shape[1]

    def spans(p):
        found, done = [], 0
        while done < units:
            chunk, at = divmod(p * units + done, depth)
            count = min(units - done, depth - at)
            found.append((done, count, chunk, at))
            done += count
        return found

    def piece_copies(p):
        pairs = []
        for done, count, chunk, at in spans(p):
            for k in range(2):
                pairs.append((piece_refs[p].at[pl.ds(k * units + done, count)], gate_up.at[chunk, pl.ds(k * depth + at, count)]))
            pairs.append((piece_refs[p].at[pl.ds(2 * units + done, count)], down.at[chunk, pl.ds(at, count)]))
        return [pltpu.make_async_copy(a, b, w_sem.at[p, i]) for i, (a, b) in enumerate(pairs)]

    x_copies, at = [], 0
    for i, ref in enumerate(x_refs):
        x_copies.append(pltpu.make_async_copy(ref, x.at[pl.ds(at, ref.shape[0])], x_sem.at[i]))
        at += ref.shape[0]

    def acc_copy(r):
        source = acc_ref.at[pl.ds(pl.multiple_of(acc_at + r * tile, tile), tile)]
        return pltpu.make_async_copy(source, total.at[pl.ds(pl.multiple_of(r * tile, tile), tile)], acc_sem.at[r])

    for copy in x_copies:
        copy.start()
    for p in range(n_pieces):
        for copy in piece_copies(p):
            copy.start()
        if p == 0 and acc_at is not None:
            for r in range(rows // tile):
                acc_copy(r).start()
    used = n_pieces * units - (n_chunks - 1) * depth
    if used < depth:
        zeros = jnp.zeros((depth - used, width), BF16)
        gate_up[n_chunks - 1, used:depth, :] = zeros
        gate_up[n_chunks - 1, depth + used :, :] = zeros
        down[n_chunks - 1, used:, :] = zeros
    for copy in x_copies:
        copy.wait()

    def store(i, first):
        count, dtype = outs[i]
        if dtype == F32:
            source = total.at[pl.ds(first, count)]
        else:
            stage[first : first + count] = total[first : first + count].astype(BF16)
            source = stage.at[pl.ds(first, count)]
        return pltpu.make_async_copy(source, out_refs[i], out_sem.at[i])

    def part_store(r):
        at = pl.ds(pl.multiple_of(r * tile, tile), tile)
        return pltpu.make_async_copy(total.at[at], out_refs[0].at[at], out_sem.at[r])

    stores = []
    waited = 0
    for c in range(n_chunks):
        while waited < n_pieces and waited * units < (c + 1) * depth:
            for copy in piece_copies(waited):
                copy.wait()
            if teacher[waited]:
                for _, count, chunk, at in spans(waited):
                    down[chunk, at : at + count, :] = -down[chunk, at : at + count, :]
            waited += 1

        def step(r, c=c):
            at = pl.ds(pl.multiple_of(r * tile, tile), tile)
            if c == 0 and acc_at is not None:
                acc_copy(r).wait()
            rows_in = x[at, :]
            turned = (((1,), (1,)), ((), ()))
            gate = lax.dot_general(rows_in, gate_up[c, :depth], turned, preferred_element_type=F32)
            up = lax.dot_general(rows_in, gate_up[c, depth:], turned, preferred_element_type=F32)
            hidden = (gate / (1.0 + jnp.exp(-gate)) * up).astype(BF16)
            term = jnp.dot(hidden, down[c], preferred_element_type=F32)
            if c == 0 and acc_at is None:
                total[at, :] = term
            else:
                total[at, :] += term
            if c == n_chunks - 1 and not unrolled:
                part_store(r).start()

        if unrolled:
            done = 0
            for r in range(rows // tile):
                step(r)
                if c == n_chunks - 1:
                    while len(stores) < len(outs) and done + outs[len(stores)][0] <= (r + 1) * tile:
                        stores.append(store(len(stores), done))
                        stores[-1].start()
                        done += outs[len(stores) - 1][0]
        else:
            pl.loop(0, rows // tile)(step)
    if not unrolled:
        stores = [part_store(r) for r in range(rows // tile)]
    for copy in stores:
        copy.wait()


def net(xs, pieces, outs, depth, tile, acc=None, acc_at=None, unrolled=True):
    rows, width = sum(a.shape[0] for a in xs), xs[0].shape[1]
    n = len(pieces)
    units = pieces[0][0].shape[0] // 3
    n_chunks = -(-n * units // depth)
    operands = list(xs) + [p for p, _ in pieces] + ([] if acc is None else [acc])
    tiles = rows // tile
    return pl.pallas_call(
        functools.partial(net_kernel, len(xs), tuple(t for _, t in pieces), acc_at, tuple(outs), tile, unrolled),
        out_shape=[jax.ShapeDtypeStruct((r, width), d) for r, d in outs],
        in_specs=whole(len(operands), pltpu.HBM),
        out_specs=whole(len(outs), pltpu.HBM),
        scratch_shapes=[
            pltpu.VMEM((rows, width), BF16),
            pltpu.VMEM((n_chunks, 2 * depth, width), BF16),
            pltpu.VMEM((n_chunks, depth, width), BF16),
            pltpu.VMEM((rows, width), F32),
            pltpu.VMEM((rows if unrolled else 16, width), BF16),
            pltpu.SemaphoreType.DMA((len(xs),)),
            pltpu.SemaphoreType.DMA((n, 6)),
            pltpu.SemaphoreType.DMA((tiles,)),
            pltpu.SemaphoreType.DMA((max(len(outs), tiles),)),
        ],
        compiler_params=params(),
        cost_estimate=pl.CostEstimate(
            flops=rows * width * units * n * 6,
            bytes_accessed=rows * width * 8 + n * 1_700_000,
            transcendentals=rows * units * n,
        ),
        name="networks",
    )(*operands)


def per_device(tokens, routes, gate_num, student_gate, student_up, student_down, teacher_gate, teacher_up, teacher_down):
    here = lax.axis_index("expert").astype(jnp.int32).reshape(1)
    routes, gate_num = routes.T, gate_num.T
    block = EXPERTS * CAP
    half = block // 2

    student = pack(student_gate[0], student_up[0], student_down[0])
    student_next = send(student, ring(1, True))
    student_prev = send(student, ring(-1, True))

    routes, student = barrier(routes, student)
    out_blocks = dispatch(here, routes, tokens)
    got = [send(out_blocks[d], hop(d)) for d in range(1, EXPERTS)]
    teacher_gate, got[0] = barrier(teacher_gate, got[0])
    teacher = pack(teacher_gate[0], teacher_up[0], teacher_down[0])
    rows = jnp.concatenate([out_blocks[0]] + got, axis=0)

    rows, teacher, student_next, student_prev = barrier(rows, teacher, student_next, student_prev)
    rows_from_prev = send(rows, ring(1, False))
    rows_from_next = send(rows, ring(-1, False))
    teacher_prev = send(teacher, ring(-1, True))
    teacher_next = send(teacher, ring(1, True))
    far_a = send(rows_from_prev[:half], ring(1, False))
    far_b = send(rows_from_next[half:], ring(-1, False))
    routes, gate_num, rows_from_prev = barrier(routes, gate_num, rows_from_prev)
    high, low = shares(here, routes, gate_num)

    student_next, teacher_prev, teacher_next, student_prev = barrier(student_next, teacher_prev, teacher_next, student_prev)
    student_far = send(student_next, ring(1, True))
    teacher_far = send(teacher_prev, ring(-1, True))

    near = [(student, False), (teacher, True), (student_next, False), (student_prev, False), (teacher_next, True), (teacher_prev, True)]
    far = [(student_far, False), (teacher_far, True)]
    (partial,) = net(
        [far_a, far_b, rows_from_next, rows_from_prev, rows], near, [(4 * block, F32)], 1024, 2 * block, unrolled=False
    )
    far_out_a, far_out_b = net([far_a, far_b], far, [(half, BF16), (half, BF16)], 640, block, partial, 0)
    sum_a = send(far_out_a, ring(1, False))
    sum_b = send(far_out_b, ring(-1, False))
    next_a, next_b, prev_a, prev_b, own = net(
        [rows_from_next, rows_from_prev, rows],
        far,
        [(half, F32), (half, BF16), (half, BF16), (half, F32), (block, F32)],
        640,
        block,
        partial,
        block,
    )
    next_b = send(next_b, ring(1, False))
    prev_a = send(prev_a, ring(-1, False))
    next_a = send((next_a + sum_a.astype(F32)).astype(BF16), ring(1, False))
    prev_b = send((prev_b + sum_b.astype(F32)).astype(BF16), ring(-1, False))
    mine_a = (own[:half] + next_a.astype(F32) + prev_a.astype(F32)).astype(BF16)
    mine_b = (own[half:] + next_b.astype(F32) + prev_b.astype(F32)).astype(BF16)
    per_half = EXPERTS // 2
    blocks = [m[d * CAP : (d + 1) * CAP] for m in (mine_a, mine_b) for d in range(per_half)]
    back = [blocks[0]] + [send(blocks[d], hop(d, True)) for d in range(1, EXPERTS)]
    return combine(high, low, back)


def solution(mesh):
    in_specs = (
        P(("expert", "shard"), None),
        P(("expert", "shard"), None),
        P(("expert", "shard"), None),
        P("expert", None, "shard"),
        P("expert", None, "shard"),
        P("expert", "shard", None),
        P("expert", None, "shard"),
        P("expert", None, "shard"),
        P("expert", "shard", None),
    )
    out_specs = P(("expert", "shard"), None)
    return jax.shard_map(
        per_device, mesh=mesh, in_specs=in_specs, out_specs=out_specs, check_vma=False
    )
```

```python
import functools

import jax
import jax.numpy as jnp
from jax import lax
from jax.experimental import pallas as pl
from jax.experimental.pallas import tpu as pltpu
from jax.sharding import PartitionSpec as P

AXES = ("expert", "shard")
BF16 = jnp.bfloat16
F32 = jnp.float32
CAP = 48
EXPERTS = 8
VMEM_LIMIT = 16 * 1024 * 1024


def dev(z, c, y, x):
    return ((z % 4 * 2 + c % 2) * 4 + y % 4) * 4 + x % 4


COORDS = [(z, c, y, x) for z in range(4) for c in range(2) for y in range(4) for x in range(4)]


def ring(step, weights):
    return [
        (dev(z, c, y, x), dev(z, c, y, x + step) if (c == 0) == weights else dev(z, c, y + step, x))
        for z, c, y, x in COORDS
    ]


def send(value, pairs):
    return lax.ppermute(value, AXES, pairs)


def barrier(*values):
    return lax.optimization_barrier(values)


def whole(count, space=pltpu.VMEM):
    return [pl.BlockSpec(memory_space=space)] * count


def params(limit=VMEM_LIMIT):
    return pltpu.CompilerParams(vmem_limit_bytes=limit)


def near(value):
    return pltpu.with_memory_space_constraint(value, pltpu.VMEM)


def places(routes_ref):
    tokens = routes_ref.shape[1]
    first, second = routes_ref[0:1, :], routes_ref[1:2, :]
    expert = lax.broadcasted_iota(jnp.int32, (16, tokens), 0)
    named = ((expert == first).astype(F32) + (expert == second).astype(F32)).astype(BF16)
    before = lax.broadcasted_iota(jnp.int32, (tokens, tokens), 0) < lax.broadcasted_iota(jnp.int32, (tokens, tokens), 1)
    earlier = jnp.dot(named, before.astype(F32).astype(BF16), preferred_element_type=F32)
    found = []
    for ids, extra in ((first, 0), (second, (first == second).astype(jnp.int32))):
        slot = jnp.sum(jnp.where(expert == ids, earlier, 0.0), axis=0, keepdims=True).astype(jnp.int32) + extra
        found.append(ids * CAP + slot)
    return found


def prepare_kernel(routes_ref, tokens_ref, *refs):
    weight_refs, packed_refs, rows_ref = refs[:6], refs[6:8], refs[8]
    held, sems = refs[9:]
    units = weight_refs[0].shape[0]
    ins = [
        pltpu.make_async_copy(ref, held.at[pl.ds(i * units, units)], sems.at[i]) for i, ref in enumerate(weight_refs)
    ]
    outs = [
        pltpu.make_async_copy(held.at[pl.ds(3 * n * units, 3 * units)], ref, sems.at[6 + n]) for n, ref in enumerate(packed_refs)
    ]
    for copy in ins:
        copy.start()
    first, second = places(routes_ref)
    slots = lax.broadcasted_iota(jnp.int32, (EXPERTS * CAP, tokens_ref.shape[0]), 0)
    chosen = ((slots == first) | (slots == second)).astype(F32).astype(BF16)
    rows_ref[...] = jnp.dot(chosen, tokens_ref[...], preferred_element_type=F32).astype(BF16)
    for n in range(2):
        for copy in ins[3 * n : 3 * n + 3]:
            copy.wait()
        outs[n].start()
    for copy in outs:
        copy.wait()


def prepare(routes, tokens, student, teacher):
    units, width = student[2].shape
    packed = jax.ShapeDtypeStruct((3 * units, width), BF16)
    return pl.pallas_call(
        prepare_kernel,
        out_shape=[packed, packed, jax.ShapeDtypeStruct((EXPERTS * CAP, width), BF16)],
        in_specs=whole(2) + whole(6, pltpu.HBM),
        out_specs=whole(2, pltpu.HBM) + whole(1),
        scratch_shapes=[pltpu.VMEM((6 * units, width), BF16), pltpu.SemaphoreType.DMA((8,))],
        compiler_params=params(63 * 1024 * 1024),
        cost_estimate=pl.CostEstimate(flops=100_000_000, bytes_accessed=7_000_000, transcendentals=0),
        name="pack_weights_dispatch_rows",
    )(routes, tokens, student[0].T, student[1].T, student[2], teacher[0].T, teacher[1].T, teacher[2])


def shares_kernel(routes_ref, gates_ref, high_ref, low_ref):
    first, second = places(routes_ref)
    gates = gates_ref[...].astype(F32)
    share = gates / jnp.sum(gates, axis=0, keepdims=True)
    slots = lax.broadcasted_iota(jnp.int32, (EXPERTS * CAP, routes_ref.shape[1]), 0)
    weight = jnp.where(slots == first, share[0:1], 0.0) + jnp.where(slots == second, share[1:2], 0.0)
    weight = weight.T
    high = weight.astype(BF16)
    high_ref[...] = high
    low_ref[...] = (weight - high.astype(F32)).astype(BF16)


def shares(routes, gates):
    tokens = routes.shape[1]
    return pl.pallas_call(
        shares_kernel,
        out_shape=[jax.ShapeDtypeStruct((tokens, EXPERTS * CAP), BF16)] * 2,
        in_specs=whole(2),
        out_specs=whole(2),
        compiler_params=params(),
        cost_estimate=pl.CostEstimate(flops=10_000_000, bytes_accessed=1_000_000, transcendentals=0),
        name="gate_shares",
    )(routes, gates)


def combine_kernel(high_ref, low_ref, rows_ref, out_ref):
    rows = rows_ref[...]
    total = jnp.dot(high_ref[...], rows, preferred_element_type=F32)
    total += jnp.dot(low_ref[...], rows, preferred_element_type=F32)
    out_ref[...] = total.astype(BF16)


def combine(high, low, rows):
    tokens, width = high.shape[0], rows.shape[1]
    return pl.pallas_call(
        combine_kernel,
        out_shape=jax.ShapeDtypeStruct((tokens, width), BF16),
        in_specs=whole(3),
        out_specs=pl.BlockSpec(memory_space=pltpu.VMEM),
        compiler_params=params(),
        cost_estimate=pl.CostEstimate(flops=200_000_000, bytes_accessed=1_000_000, transcendentals=0),
        name="combine_rows",
    )(high, low, rows)


def net_kernel(n_x, pieces, depths, acc_at, outs, tile, *refs):
    x_refs, refs = refs[:n_x], refs[n_x:]
    piece_refs, refs = refs[: len(pieces)], refs[len(pieces) :]
    if acc_at is not None:
        acc_ref, refs = refs[0], refs[1:]
    out_refs, refs = refs[: len(outs)], refs[len(outs) :]
    x, gate_up, down, x_sem, w_sem = refs
    rows, width = x.shape
    units = piece_refs[0].shape[0] // 3
    starts = [sum(depths[:c]) for c in range(len(depths))]

    wide_pairs, down_pairs, negative = ([[] for _ in depths] for _ in range(3))
    at = 0
    for ref, (teacher, first, count) in zip(piece_refs, pieces):
        done = 0
        while done < count:
            chunk = max(c for c in range(len(depths)) if starts[c] <= at)
            n = min(count - done, starts[chunk] + depths[chunk] - at)
            inside = at - starts[chunk]
            for k in range(2):
                to = 2 * starts[chunk] + k * depths[chunk] + inside
                wide_pairs[chunk].append((ref.at[pl.ds(k * units + first + done, n)], gate_up.at[pl.ds(to, n)]))
            down_pairs[chunk].append((ref.at[pl.ds(2 * units + first + done, n)], down.at[pl.ds(at, n)]))
            if teacher:
                negative[chunk].append((at, n))
            at += n
            done += n
    used = at

    def copies_of(pairs, base):
        return [pltpu.make_async_copy(a, b, w_sem.at[base + i]) for i, (a, b) in enumerate(pairs)]

    wide_copies, down_copies, base = [], [], 0
    for c in range(len(depths)):
        wide_copies.append(copies_of(wide_pairs[c], base))
        base += len(wide_pairs[c])
        down_copies.append(copies_of(down_pairs[c], base))
        base += len(down_pairs[c])

    x_copies, at = [], 0
    for i, ref in enumerate(x_refs):
        x_copies.append(pltpu.make_async_copy(ref, x.at[pl.ds(at, ref.shape[0])], x_sem.at[i]))
        at += ref.shape[0]

    for copy in x_copies:
        copy.start()
    for c in range(len(depths)):
        for copy in wide_copies[c] + down_copies[c]:
            copy.start()
    if used < sum(depths):
        c = len(depths) - 1
        empty = sum(depths) - used
        zeros = jnp.zeros((empty, width), BF16)
        for k in range(2):
            end = 2 * starts[c] + (k + 1) * depths[c]
            gate_up[end - empty : end, :] = zeros
        down[used:, :] = zeros
    for copy in x_copies:
        copy.wait()

    for c, depth in enumerate(depths):
        for copy in wide_copies[c]:
            copy.wait()

        @pl.loop(0, rows // tile)
        def _(r, c=c, depth=depth):
            at = pl.ds(pl.multiple_of(r * tile, tile), tile)
            low = 2 * starts[c]
            rows_in = x[at, :]
            turned = (((1,), (1,)), ((), ()))
            gate = lax.dot_general(rows_in, gate_up[low : low + depth], turned, preferred_element_type=F32)
            up = lax.dot_general(rows_in, gate_up[low + depth : low + 2 * depth], turned, preferred_element_type=F32)
            hidden = (gate / (1.0 + jnp.exp(-gate)) * up).astype(BF16)

            @pl.when(r == 0)
            def _():
                for copy in down_copies[c]:
                    copy.wait()
                for first, n in negative[c]:
                    down[first : first + n, :] = -down[first : first + n, :]

            term = jnp.dot(hidden, down[starts[c] : starts[c] + depth], preferred_element_type=F32)
            if acc_at is not None:
                term += acc_ref[pl.ds(pl.multiple_of(acc_at + r * tile, tile), tile), :]
            if len(outs) == 1 and c > 0:
                out_refs[0][at, :] += term
            elif len(outs) == 1:
                out_refs[0][at, :] = term.astype(outs[0])
            else:
                for i, dtype in enumerate(outs):

                    @pl.when(r == i)
                    def _(i=i, dtype=dtype):
                        out_refs[i][...] = term.astype(dtype)


def net(xs, pieces, depths, outs, tile, limit, acc=None, acc_at=None):
    rows, width = sum(a.shape[0] for a in xs), xs[0].shape[1]
    hidden = sum(depths)
    assert acc is None or len(depths) == 1
    operands = list(xs) + [p[0] for p in pieces] + ([] if acc is None else [acc])
    return pl.pallas_call(
        functools.partial(net_kernel, len(xs), tuple(p[1:] for p in pieces), tuple(depths), acc_at, tuple(outs), tile),
        out_shape=[pltpu.VMEM((rows // len(outs), width), d) for d in outs],
        in_specs=whole(len(operands)),
        out_specs=whole(len(outs)),
        scratch_shapes=[
            pltpu.VMEM((rows, width), BF16),
            pltpu.VMEM((2 * hidden, width), BF16),
            pltpu.VMEM((hidden, width), BF16),
            pltpu.SemaphoreType.DMA((len(xs),)),
            pltpu.SemaphoreType.DMA((len(pieces) * 6,)),
        ],
        compiler_params=params(limit),
        cost_estimate=pl.CostEstimate(
            flops=rows * width * hidden * 6, bytes_accessed=rows * width * 8 + hidden * width * 6, transcendentals=rows * hidden
        ),
        name="networks",
    )(*(near(a) for a in operands))


def per_device(tokens, routes, gate_num, student_gate, student_up, student_down, teacher_gate, teacher_up, teacher_down):
    routes, gate_num = routes.T, gate_num.T
    width = tokens.shape[1]
    units = student_gate.shape[2]
    block = EXPERTS * CAP
    half = block // 2

    def exchange(value):
        value = value.reshape(EXPERTS, CAP, width)
        return lax.all_to_all(value, "expert", split_axis=0, concat_axis=0, tiled=True).reshape(block, width)

    student, teacher, rows = prepare(
        routes, tokens, (student_gate[0], student_up[0], student_down[0]), (teacher_gate[0], teacher_up[0], teacher_down[0])
    )
    from_prev_student = send(student, ring(1, True))
    from_next_student = send(student, ring(-1, True))
    rows = exchange(rows)

    rows, teacher, from_prev_student, from_next_student = barrier(rows, teacher, from_prev_student, from_next_student)
    far_student = send(from_prev_student, ring(1, True))
    from_next_teacher = send(teacher, ring(-1, True))
    rows_from_prev = send(rows, ring(1, False))
    rows_from_next = send(rows, ring(-1, False))
    far_a = send(rows_from_prev[:half], ring(1, False))
    far_b = send(rows_from_next[half:], ring(-1, False))
    teacher, far_student, from_next_teacher = barrier(teacher, far_student, from_next_teacher)
    from_prev_teacher = send(teacher, ring(1, True))
    far_teacher = send(from_next_teacher, ring(-1, True))
    high, low = shares(routes, gate_num)

    xs = [far_a, far_b, rows_from_next, rows_from_prev, rows]
    part = units - 32
    early = [
        (student, False, 0, units),
        (teacher, True, 0, units),
        (from_prev_student, False, 0, units),
        (from_next_student, False, 0, units),
        (far_student, False, 0, units),
        (from_next_teacher, True, 0, part),
    ]
    (partial,) = net(xs, early, [768, 1024], [F32], 2 * block, 32 * 1024 * 1024)
    late = [(from_next_teacher, True, part, units - part), (from_prev_teacher, True, 0, units), (far_teacher, True, 0, units)]
    (out_far,) = net(xs[:2], late, [640], [BF16], block, 14 * 1024 * 1024, partial, 0)
    partial, out_far = barrier(partial, out_far)
    out_far = send(out_far, ring(2, False))
    to_next, to_prev, own = net(xs[2:], late, [640], [BF16, BF16, F32], block, 14 * 1024 * 1024, partial, block)
    from_prev = send(to_next, ring(1, False))
    from_next = send(to_prev, ring(-1, False))
    mine = own + from_prev.astype(F32) + from_next.astype(F32) + out_far.astype(F32)
    return combine(high, low, exchange(mine.astype(BF16)))


def solution(mesh):
    in_specs = (
        P(("expert", "shard"), None),
        P(("expert", "shard"), None),
        P(("expert", "shard"), None),
        P("expert", None, "shard"),
        P("expert", None, "shard"),
        P("expert", "shard", None),
        P("expert", None, "shard"),
        P("expert", None, "shard"),
        P("expert", "shard", None),
    )
    out_specs = P(("expert", "shard"), None)
    return jax.shard_map(
        per_device, mesh=mesh, in_specs=in_specs, out_specs=out_specs, check_vma=False
    )
```

```python
import functools

import jax
import jax.numpy as jnp
from jax import lax
from jax.experimental import pallas as pl
from jax.experimental.pallas import tpu as pltpu
from jax.sharding import PartitionSpec as P

AXES = ("expert", "shard")
BF16 = jnp.bfloat16
F32 = jnp.float32
CAP = 48
EXPERTS = 8
VMEM_LIMIT = 16 * 1024 * 1024


def dev(z, c, y, x):
    return ((z % 4 * 2 + c % 2) * 4 + y % 4) * 4 + x % 4


COORDS = [(z, c, y, x) for z in range(4) for c in range(2) for y in range(4) for x in range(4)]


def ring(step, weights):
    return [
        (dev(z, c, y, x), dev(z, c, y, x + step) if (c == 0) == weights else dev(z, c, y + step, x))
        for z, c, y, x in COORDS
    ]


def hop(offset, back=False):
    dz, dc = offset // 2, offset % 2
    pairs = [(dev(z, c, y, x), dev(z + dz, c + dc, y, x)) for z, c, y, x in COORDS]
    return [(b, a) for a, b in pairs] if back else pairs


def send(value, pairs):
    return lax.ppermute(value, AXES, pairs)


def barrier(*values):
    return lax.optimization_barrier(values)


def whole(count, space=pltpu.VMEM):
    return [pl.BlockSpec(memory_space=space)] * count


def params(limit=VMEM_LIMIT):
    return pltpu.CompilerParams(vmem_limit_bytes=limit)


def near(value):
    return pltpu.with_memory_space_constraint(value, pltpu.VMEM)


def places(routes_ref):
    tokens = routes_ref.shape[1]
    first, second = routes_ref[0:1, :], routes_ref[1:2, :]
    expert = lax.broadcasted_iota(jnp.int32, (16, tokens), 0)
    named = ((expert == first).astype(F32) + (expert == second).astype(F32)).astype(BF16)
    before = lax.broadcasted_iota(jnp.int32, (tokens, tokens), 0) < lax.broadcasted_iota(jnp.int32, (tokens, tokens), 1)
    earlier = jnp.dot(named, before.astype(F32).astype(BF16), preferred_element_type=F32)
    found = []
    for ids, extra in ((first, 0), (second, (first == second).astype(jnp.int32))):
        slot = jnp.sum(jnp.where(expert == ids, earlier, 0.0), axis=0, keepdims=True).astype(jnp.int32) + extra
        found.append(ids * CAP + slot)
    return found


def pack_kernel(n_rest, *refs):
    weight_refs, rest, packed_ref = refs[:3], refs[3 : 3 + n_rest], refs[3 + n_rest]
    sems = refs[-1]
    units = weight_refs[0].shape[0]
    ins = [
        pltpu.make_async_copy(ref, packed_ref.at[pl.ds(i * units, units)], sems.at[i]) for i, ref in enumerate(weight_refs)
    ]
    for copy in ins:
        copy.start()
    if rest:
        routes_ref, tokens_ref = rest
        first, second = places(routes_ref)
        slots = lax.broadcasted_iota(jnp.int32, (EXPERTS * CAP, tokens_ref.shape[0]), 0)
        chosen = ((slots == first) | (slots == second)).astype(F32).astype(BF16)
        refs[4 + n_rest][...] = jnp.dot(chosen, tokens_ref[...], preferred_element_type=F32).astype(BF16)
    for copy in ins:
        copy.wait()


def pack(weights, *rest):
    gate, up, down = weights
    units, width = down.shape
    rows = [pltpu.VMEM((EXPERTS * CAP, width), BF16)] if rest else []
    return pl.pallas_call(
        functools.partial(pack_kernel, len(rest)),
        out_shape=[pltpu.VMEM((3 * units, width), BF16)] + rows,
        in_specs=whole(3, pltpu.HBM) + whole(len(rest)),
        out_specs=whole(1 + len(rows)),
        scratch_shapes=[pltpu.SemaphoreType.DMA((3,))],
        compiler_params=params(58 * 1024 * 1024 if rest else VMEM_LIMIT),
        cost_estimate=pl.CostEstimate(flops=100_000_000, bytes_accessed=4_000_000, transcendentals=0),
        name="pack_weights",
    )(gate.T, up.T, down, *rest)


def shares_kernel(routes_ref, gates_ref, high_ref, low_ref):
    first, second = places(routes_ref)
    gates = gates_ref[...].astype(F32)
    share = gates / jnp.sum(gates, axis=0, keepdims=True)
    slots = lax.broadcasted_iota(jnp.int32, (EXPERTS * CAP, routes_ref.shape[1]), 0)
    weight = jnp.where(slots == first, share[0:1], 0.0) + jnp.where(slots == second, share[1:2], 0.0)
    weight = weight.T
    high = weight.astype(BF16)
    high_ref[...] = high
    low_ref[...] = (weight - high.astype(F32)).astype(BF16)


def shares(routes, gates):
    tokens = routes.shape[1]
    return pl.pallas_call(
        shares_kernel,
        out_shape=[jax.ShapeDtypeStruct((tokens, EXPERTS * CAP), BF16)] * 2,
        in_specs=whole(2),
        out_specs=whole(2),
        compiler_params=params(),
        cost_estimate=pl.CostEstimate(flops=10_000_000, bytes_accessed=1_000_000, transcendentals=0),
        name="gate_shares",
    )(routes, gates)


def expert_at(here, offset, sign):
    return (((here >> 1) + sign * (offset // 2)) & 3) * 2 + ((here + offset % 2) & 1)


def sum_kernel(here_ref, own_ref, prev_a_ref, prev_b_ref, next_a_ref, next_b_ref, *refs):
    *out_refs, total = refs
    half = prev_a_ref.shape[0]
    total[:half] = own_ref[:half] + prev_a_ref[...].astype(F32) + next_a_ref[...].astype(F32)
    total[half:] = own_ref[half:] + prev_b_ref[...].astype(F32) + next_b_ref[...].astype(F32)
    for offset, out_ref in enumerate(out_refs):
        at = pl.multiple_of(expert_at(here_ref[0], offset, -1) * CAP, CAP)
        out_ref[...] = total[pl.ds(at, CAP), :].astype(BF16)


def sum_rows(here, own, *parts):
    rows, width = own.shape
    return pl.pallas_call(
        sum_kernel,
        out_shape=[pltpu.VMEM((CAP, width), BF16)] * EXPERTS,
        in_specs=whole(1, pltpu.SMEM) + whole(5),
        out_specs=whole(EXPERTS),
        scratch_shapes=[pltpu.VMEM((rows, width), F32)],
        compiler_params=params(),
        cost_estimate=pl.CostEstimate(flops=1_000_000, bytes_accessed=4_000_000, transcendentals=0),
        name="sum_rows",
    )(here, near(own), *(near(p) for p in parts))


def combine_kernel(here_ref, high_ref, low_ref, *refs):
    *block_refs, out_ref, held = refs
    for offset, ref in enumerate(block_refs):
        at = pl.multiple_of(expert_at(here_ref[0], offset, 1) * CAP, CAP)
        held[pl.ds(at, CAP), :] = ref[...]
    rows = held[...]
    total = jnp.dot(high_ref[...], rows, preferred_element_type=F32)
    total += jnp.dot(low_ref[...], rows, preferred_element_type=F32)
    out_ref[...] = total.astype(BF16)


def combine(here, high, low, blocks):
    tokens, width = high.shape[0], blocks[0].shape[1]
    return pl.pallas_call(
        combine_kernel,
        out_shape=jax.ShapeDtypeStruct((tokens, width), BF16),
        in_specs=whole(1, pltpu.SMEM) + whole(2 + EXPERTS),
        out_specs=pl.BlockSpec(memory_space=pltpu.VMEM),
        scratch_shapes=[pltpu.VMEM((EXPERTS * CAP, width), BF16)],
        compiler_params=params(),
        cost_estimate=pl.CostEstimate(flops=200_000_000, bytes_accessed=1_000_000, transcendentals=0),
        name="combine_rows",
    )(here, near(high), near(low), *(near(b) for b in blocks))


def net_kernel(n_x, pieces, depths, sum_at, add, outs, tile, *refs):
    x_refs, refs = refs[:n_x], refs[n_x:]
    piece_refs, refs = refs[: len(pieces)], refs[len(pieces) :]
    n_sums = len(refs) - max(len(outs), 1) - 5
    if n_sums:
        acc_ref, refs = refs[0], refs[1:]
    if outs:
        out_refs, refs = refs[: len(outs)], refs[len(outs) :]
    else:
        sum_ref, refs = refs[0], refs[1:]
    x, gate_up, down, x_sem, w_sem = refs
    rows, width = x.shape
    units = piece_refs[0].shape[0] // 3
    starts = [sum(depths[:c]) for c in range(len(depths))]

    wide_pairs, down_pairs, negative = ([[] for _ in depths] for _ in range(3))
    at = 0
    for ref, (teacher, first, count) in zip(piece_refs, pieces):
        done = 0
        while done < count:
            chunk = max(c for c in range(len(depths)) if starts[c] <= at)
            n = min(count - done, starts[chunk] + depths[chunk] - at)
            inside = at - starts[chunk]
            for k in range(2):
                to = 2 * starts[chunk] + k * depths[chunk] + inside
                wide_pairs[chunk].append((ref.at[pl.ds(k * units + first + done, n)], gate_up.at[pl.ds(to, n)]))
            down_pairs[chunk].append((ref.at[pl.ds(2 * units + first + done, n)], down.at[pl.ds(at, n)]))
            if teacher:
                negative[chunk].append((at, n))
            at += n
            done += n
    used = at

    def copies_of(pairs, base):
        return [pltpu.make_async_copy(a, b, w_sem.at[base + i]) for i, (a, b) in enumerate(pairs)]

    wide_copies, down_copies, base = [], [], 0
    for c in range(len(depths)):
        wide_copies.append(copies_of(wide_pairs[c], base))
        base += len(wide_pairs[c])
        down_copies.append(copies_of(down_pairs[c], base))
        base += len(down_pairs[c])

    x_copies, at = [], 0
    for i, ref in enumerate(x_refs):
        x_copies.append(pltpu.make_async_copy(ref, x.at[pl.ds(at, ref.shape[0])], x_sem.at[i]))
        at += ref.shape[0]

    for copy in x_copies:
        copy.start()
    for c in range(len(depths)):
        for copy in wide_copies[c] + down_copies[c]:
            copy.start()
    if used < sum(depths):
        c = len(depths) - 1
        empty = sum(depths) - used
        zeros = jnp.zeros((empty, width), BF16)
        for k in range(2):
            end = 2 * starts[c] + (k + 1) * depths[c]
            gate_up[end - empty : end, :] = zeros
        down[used:, :] = zeros
    for copy in x_copies:
        copy.wait()

    for c, depth in enumerate(depths):
        for copy in wide_copies[c]:
            copy.wait()

        @pl.loop(0, rows // tile)
        def _(r, c=c, depth=depth):
            at = pl.ds(pl.multiple_of(r * tile, tile), tile)
            low = 2 * starts[c]
            rows_in = x[at, :]
            turned = (((1,), (1,)), ((), ()))
            gate = lax.dot_general(rows_in, gate_up[low : low + depth], turned, preferred_element_type=F32)
            up = lax.dot_general(rows_in, gate_up[low + depth : low + 2 * depth], turned, preferred_element_type=F32)
            hidden = (gate / (1.0 + jnp.exp(-gate)) * up).astype(BF16)

            @pl.when(r == 0)
            def _():
                for copy in down_copies[c]:
                    copy.wait()
                for first, n in negative[c]:
                    down[first : first + n, :] = -down[first : first + n, :]

            term = jnp.dot(hidden, down[starts[c] : starts[c] + depth], preferred_element_type=F32)
            within = pl.ds(pl.multiple_of(sum_at + r * tile, tile), tile)
            if not outs and (add or c > 0):
                sum_ref[within, :] += term
            elif not outs:
                sum_ref[within, :] = term
            else:
                term += acc_ref[within, :]
                ends = [sum(n for n, _ in outs[: i + 1]) for i in range(len(outs))]
                for t in range(rows // tile):

                    @pl.when(r == t)
                    def _(t=t):
                        for (n, dtype), end, ref in zip(outs, ends, out_refs):
                            if t * tile < end <= (t + 1) * tile:
                                ref[...] = term[end - n - t * tile : end - t * tile].astype(dtype)


def net(xs, pieces, depths, tile, limit, total, total_at, add, outs=()):
    rows, width = sum(a.shape[0] for a in xs), xs[0].shape[1]
    fresh = isinstance(total, int)
    hidden = sum(depths)
    assert not outs or len(depths) == 1
    operands = list(xs) + [p[0] for p in pieces] + ([] if fresh else [total])
    shapes = outs or [(total if fresh else total.shape[0], F32)]
    return pl.pallas_call(
        functools.partial(net_kernel, len(xs), tuple(p[1:] for p in pieces), tuple(depths), total_at, add, tuple(outs), tile),
        out_shape=[pltpu.VMEM((n, width), d) for n, d in shapes],
        in_specs=whole(len(operands)),
        out_specs=whole(len(shapes)),
        input_output_aliases={} if fresh or outs else {len(operands) - 1: 0},
        scratch_shapes=[
            pltpu.VMEM((rows, width), BF16),
            pltpu.VMEM((2 * hidden, width), BF16),
            pltpu.VMEM((hidden, width), BF16),
            pltpu.SemaphoreType.DMA((len(xs),)),
            pltpu.SemaphoreType.DMA((len(pieces) * 6,)),
        ],
        compiler_params=params(limit),
        cost_estimate=pl.CostEstimate(
            flops=rows * width * hidden * 6, bytes_accessed=rows * width * 8 + hidden * width * 6, transcendentals=rows * hidden
        ),
        name="networks",
    )(*(near(a) for a in operands))


def per_device(tokens, routes, gate_num, student_gate, student_up, student_down, teacher_gate, teacher_up, teacher_down):
    here = lax.axis_index("expert").astype(jnp.int32).reshape(1)
    routes, gate_num = routes.T, gate_num.T
    width = tokens.shape[1]
    units = student_gate.shape[2]
    block = EXPERTS * CAP
    half = block // 2
    mib = 1024 * 1024

    student, rows = pack((student_gate[0], student_up[0], student_down[0]), routes, tokens)
    from_prev_student = send(student, ring(1, True))
    from_next_student = send(student, ring(-1, True))
    rows = rows.reshape(EXPERTS, CAP, width)
    rows = lax.all_to_all(rows, "expert", split_axis=0, concat_axis=0, tiled=True).reshape(block, width)

    rows_from_prev = send(rows, ring(1, False))
    rows_from_next = send(rows, ring(-1, False))

    (teacher,) = pack((barrier(teacher_gate, rows)[0][0], teacher_up[0], teacher_down[0]))
    first = [(student, False, 0, units), (teacher, True, 0, units), (from_prev_student, False, 0, units), (from_next_student, False, 0, units)]
    (total,) = net([rows], first, [512, 768], block, 28 * mib, 4 * block, 3 * block, False)

    total, from_prev_student, teacher, rows_from_prev, rows_from_next = barrier(total, from_prev_student, teacher, rows_from_prev, rows_from_next)
    near_xs = [rows_from_next, rows_from_prev]
    far_a = send(rows_from_prev[:half], ring(1, False))
    far_b = send(rows_from_next[half:], ring(-1, False))
    far_student = send(from_prev_student, ring(1, True))
    from_next_teacher = send(teacher, ring(-1, True))
    first[1] = (teacher, True, 0, units)
    first[2] = (from_prev_student, False, 0, units)
    (total,) = net(near_xs, first, [512, 768], block, 28 * mib, total, block, False)
    total, far_a, far_b = barrier(total, far_a, far_b)
    far_xs = [far_a, far_b]
    (total,) = net(far_xs, first, [512, 768], block, 28 * mib, total, 0, False)
    teacher, far_student, from_next_teacher, total = barrier(teacher, far_student, from_next_teacher, total)
    from_prev_teacher = send(teacher, ring(1, True))
    far_teacher = send(from_next_teacher, ring(-1, True))
    high, low = shares(routes, gate_num)

    second = [(far_student, False, 0, units), (from_next_teacher, True, 0, units)]
    last = [(from_prev_teacher, True, 0, units), (far_teacher, True, 0, units)]
    (total,) = net(far_xs + near_xs + [rows], second, [640], 2 * block, 24 * mib, total, 0, True)
    out_a, out_b = net(far_xs, last, [640], block, 16 * mib, total, 0, True, [(half, BF16), (half, BF16)])
    sum_a = send(out_a, ring(1, False))
    sum_b = send(out_b, ring(-1, False))
    next_a, next_b, prev_a, prev_b = net(
        near_xs, last, [640], block, 16 * mib, total, block, True, [(half, F32), (half, BF16), (half, BF16), (half, F32)]
    )
    (own,) = net([rows], last, [640], block, 16 * mib, total, 3 * block, True, [(block, F32)])
    next_b = send(next_b, ring(1, False))
    prev_a = send(prev_a, ring(-1, False))
    next_a = send((next_a + sum_a.astype(F32)).astype(BF16), ring(1, False))
    prev_b = send((prev_b + sum_b.astype(F32)).astype(BF16), ring(-1, False))
    blocks = sum_rows(here, own, next_a, next_b, prev_a, prev_b)
    return combine(here, high, low, [blocks[0]] + [send(blocks[d], hop(d, True)) for d in range(1, EXPERTS)])


def solution(mesh):
    in_specs = (
        P(("expert", "shard"), None),
        P(("expert", "shard"), None),
        P(("expert", "shard"), None),
        P("expert", None, "shard"),
        P("expert", None, "shard"),
        P("expert", "shard", None),
        P("expert", None, "shard"),
        P("expert", None, "shard"),
        P("expert", "shard", None),
    )
    out_specs = P(("expert", "shard"), None)
    return jax.shard_map(
        per_device, mesh=mesh, in_specs=in_specs, out_specs=out_specs, check_vma=False
    )
```

```python
import functools

import jax
import jax.numpy as jnp
from jax import lax
from jax.experimental import pallas as pl
from jax.experimental.pallas import tpu as pltpu
from jax.sharding import PartitionSpec as P

AXES = ("expert", "shard")
BF16 = jnp.bfloat16
F32 = jnp.float32
CAP = 48
EXPERTS = 8
VMEM_LIMIT = 16 * 1024 * 1024


def dev(z, c, y, x):
    return ((z % 4 * 2 + c % 2) * 4 + y % 4) * 4 + x % 4


COORDS = [(z, c, y, x) for z in range(4) for c in range(2) for y in range(4) for x in range(4)]


def ring(step, weights):
    return [
        (dev(z, c, y, x), dev(z, c, y, x + step) if (c == 0) == weights else dev(z, c, y + step, x))
        for z, c, y, x in COORDS
    ]


def hop(offset, back=False):
    dz, dc = offset // 2, offset % 2
    pairs = [(dev(z, c, y, x), dev(z + dz, c + dc, y, x)) for z, c, y, x in COORDS]
    return [(b, a) for a, b in pairs] if back else pairs


def send(value, pairs):
    return lax.ppermute(value, AXES, pairs)


def barrier(*values):
    return lax.optimization_barrier(values)


def whole(count, space=pltpu.VMEM):
    return [pl.BlockSpec(memory_space=space)] * count


def params(limit=VMEM_LIMIT):
    return pltpu.CompilerParams(vmem_limit_bytes=limit)


def near(value):
    return pltpu.with_memory_space_constraint(value, pltpu.VMEM)


def places(routes_ref):
    tokens = routes_ref.shape[1]
    first, second = routes_ref[0:1, :], routes_ref[1:2, :]
    expert = lax.broadcasted_iota(jnp.int32, (16, tokens), 0)
    named = ((expert == first).astype(F32) + (expert == second).astype(F32)).astype(BF16)
    before = lax.broadcasted_iota(jnp.int32, (tokens, tokens), 0) < lax.broadcasted_iota(jnp.int32, (tokens, tokens), 1)
    earlier = jnp.dot(named, before.astype(F32).astype(BF16), preferred_element_type=F32)
    found = []
    for ids, extra in ((first, 0), (second, (first == second).astype(jnp.int32))):
        slot = jnp.sum(jnp.where(expert == ids, earlier, 0.0), axis=0, keepdims=True).astype(jnp.int32) + extra
        found.append(ids * CAP + slot)
    return found


def pack_kernel(n_rest, *refs):
    weight_refs, rest, packed_ref = refs[:3], refs[3 : 3 + n_rest], refs[3 + n_rest]
    sems = refs[-1]
    units = weight_refs[0].shape[0]
    ins = [
        pltpu.make_async_copy(ref, packed_ref.at[pl.ds(i * units, units)], sems.at[i]) for i, ref in enumerate(weight_refs)
    ]
    for copy in ins:
        copy.start()
    if rest:
        routes_ref, tokens_ref = rest
        first, second = places(routes_ref)
        slots = lax.broadcasted_iota(jnp.int32, (EXPERTS * CAP, tokens_ref.shape[0]), 0)
        chosen = ((slots == first) | (slots == second)).astype(F32).astype(BF16)
        refs[4 + n_rest][...] = jnp.dot(chosen, tokens_ref[...], preferred_element_type=F32).astype(BF16)
    for copy in ins:
        copy.wait()


def pack(weights, *rest):
    gate, up, down = weights
    units, width = down.shape
    rows = [pltpu.VMEM((EXPERTS * CAP, width), BF16)] if rest else []
    return pl.pallas_call(
        functools.partial(pack_kernel, len(rest)),
        out_shape=[pltpu.VMEM((3 * units, width), BF16)] + rows,
        in_specs=whole(3, pltpu.HBM) + whole(len(rest)),
        out_specs=whole(1 + len(rows)),
        scratch_shapes=[pltpu.SemaphoreType.DMA((3,))],
        compiler_params=params(58 * 1024 * 1024 if rest else VMEM_LIMIT),
        cost_estimate=pl.CostEstimate(flops=100_000_000, bytes_accessed=4_000_000, transcendentals=0),
        name="pack_weights",
    )(gate.T, up.T, down, *rest)


def shares_kernel(routes_ref, gates_ref, high_ref, low_ref):
    first, second = places(routes_ref)
    gates = gates_ref[...].astype(F32)
    share = gates / jnp.sum(gates, axis=0, keepdims=True)
    slots = lax.broadcasted_iota(jnp.int32, (EXPERTS * CAP, routes_ref.shape[1]), 0)
    weight = jnp.where(slots == first, share[0:1], 0.0) + jnp.where(slots == second, share[1:2], 0.0)
    weight = weight.T
    high = weight.astype(BF16)
    high_ref[...] = high
    low_ref[...] = (weight - high.astype(F32)).astype(BF16)


def shares(routes, gates):
    tokens = routes.shape[1]
    return pl.pallas_call(
        shares_kernel,
        out_shape=[jax.ShapeDtypeStruct((tokens, EXPERTS * CAP), BF16)] * 2,
        in_specs=whole(2),
        out_specs=whole(2),
        compiler_params=params(),
        cost_estimate=pl.CostEstimate(flops=10_000_000, bytes_accessed=1_000_000, transcendentals=0),
        name="gate_shares",
    )(routes, gates)


def expert_at(here, offset, sign):
    return (((here >> 1) + sign * (offset // 2)) & 3) * 2 + ((here + offset % 2) & 1)


def sum_kernel(here_ref, own_ref, *refs):
    part_refs, out_refs = refs[:3], refs[3:]
    for offset, out_ref in enumerate(out_refs):
        at = pl.ds(pl.multiple_of(expert_at(here_ref[0], offset, -1) * CAP, CAP), CAP)
        total = own_ref[at, :]
        for ref in part_refs:
            total += ref[at, :].astype(F32)
        out_ref[...] = total.astype(BF16)


def sum_rows(here, own, *parts):
    width = own.shape[1]
    return pl.pallas_call(
        sum_kernel,
        out_shape=[pltpu.VMEM((CAP, width), BF16)] * EXPERTS,
        in_specs=whole(1, pltpu.SMEM) + whole(4),
        out_specs=whole(EXPERTS),
        compiler_params=params(),
        cost_estimate=pl.CostEstimate(flops=1_000_000, bytes_accessed=4_000_000, transcendentals=0),
        name="sum_rows",
    )(here, near(own), *(near(p) for p in parts))


def combine_kernel(here_ref, high_ref, low_ref, *refs):
    *block_refs, out_ref, held = refs
    for offset, ref in enumerate(block_refs):
        at = pl.multiple_of(expert_at(here_ref[0], offset, 1) * CAP, CAP)
        held[pl.ds(at, CAP), :] = ref[...]
    rows = held[...]
    total = jnp.dot(high_ref[...], rows, preferred_element_type=F32)
    total += jnp.dot(low_ref[...], rows, preferred_element_type=F32)
    out_ref[...] = total.astype(BF16)


def combine(here, high, low, blocks):
    tokens, width = high.shape[0], blocks[0].shape[1]
    return pl.pallas_call(
        combine_kernel,
        out_shape=jax.ShapeDtypeStruct((tokens, width), BF16),
        in_specs=whole(1, pltpu.SMEM) + whole(2 + EXPERTS),
        out_specs=pl.BlockSpec(memory_space=pltpu.VMEM),
        scratch_shapes=[pltpu.VMEM((EXPERTS * CAP, width), BF16)],
        compiler_params=params(),
        cost_estimate=pl.CostEstimate(flops=200_000_000, bytes_accessed=1_000_000, transcendentals=0),
        name="combine_rows",
    )(here, near(high), near(low), *(near(b) for b in blocks))


def net_kernel(n_x, pieces, depths, sum_at, add, outs, tile, *refs):
    x_refs, refs = refs[:n_x], refs[n_x:]
    piece_refs, refs = refs[: len(pieces)], refs[len(pieces) :]
    n_sums = len(refs) - max(len(outs), 1) - 5
    if n_sums:
        acc_ref, refs = refs[0], refs[1:]
    if outs:
        out_refs, refs = refs[: len(outs)], refs[len(outs) :]
    else:
        sum_ref, refs = refs[0], refs[1:]
    x, gate_up, down, x_sem, w_sem = refs
    rows, width = x.shape
    units = piece_refs[0].shape[0] // 3
    starts = [sum(depths[:c]) for c in range(len(depths))]

    wide_pairs, down_pairs, negative = ([[] for _ in depths] for _ in range(3))
    at = 0
    for ref, (teacher, first, count) in zip(piece_refs, pieces):
        done = 0
        while done < count:
            chunk = max(c for c in range(len(depths)) if starts[c] <= at)
            n = min(count - done, starts[chunk] + depths[chunk] - at)
            inside = at - starts[chunk]
            for k in range(2):
                to = 2 * starts[chunk] + k * depths[chunk] + inside
                wide_pairs[chunk].append((ref.at[pl.ds(k * units + first + done, n)], gate_up.at[pl.ds(to, n)]))
            down_pairs[chunk].append((ref.at[pl.ds(2 * units + first + done, n)], down.at[pl.ds(at, n)]))
            if teacher:
                negative[chunk].append((at, n))
            at += n
            done += n
    used = at

    def copies_of(pairs, base):
        return [pltpu.make_async_copy(a, b, w_sem.at[base + i]) for i, (a, b) in enumerate(pairs)]

    wide_copies, down_copies, base = [], [], 0
    for c in range(len(depths)):
        wide_copies.append(copies_of(wide_pairs[c], base))
        base += len(wide_pairs[c])
        down_copies.append(copies_of(down_pairs[c], base))
        base += len(down_pairs[c])

    x_copies, at = [], 0
    for i, ref in enumerate(x_refs):
        x_copies.append(pltpu.make_async_copy(ref, x.at[pl.ds(at, ref.shape[0])], x_sem.at[i]))
        at += ref.shape[0]

    for copy in x_copies:
        copy.start()
    for c in range(len(depths)):
        for copy in wide_copies[c] + down_copies[c]:
            copy.start()
    if used < sum(depths):
        c = len(depths) - 1
        empty = sum(depths) - used
        zeros = jnp.zeros((empty, width), BF16)
        for k in range(2):
            end = 2 * starts[c] + (k + 1) * depths[c]
            gate_up[end - empty : end, :] = zeros
        down[used:, :] = zeros
    for copy in x_copies:
        copy.wait()

    for c, depth in enumerate(depths):
        for copy in wide_copies[c]:
            copy.wait()

        @pl.loop(0, rows // tile)
        def _(r, c=c, depth=depth):
            at = pl.ds(pl.multiple_of(r * tile, tile), tile)
            low = 2 * starts[c]
            rows_in = x[at, :]
            turned = (((1,), (1,)), ((), ()))
            gate = lax.dot_general(rows_in, gate_up[low : low + depth], turned, preferred_element_type=F32)
            up = lax.dot_general(rows_in, gate_up[low + depth : low + 2 * depth], turned, preferred_element_type=F32)
            hidden = (gate / (1.0 + jnp.exp(-gate)) * up).astype(BF16)

            @pl.when(r == 0)
            def _():
                for copy in down_copies[c]:
                    copy.wait()
                for first, n in negative[c]:
                    down[first : first + n, :] = -down[first : first + n, :]

            term = jnp.dot(hidden, down[starts[c] : starts[c] + depth], preferred_element_type=F32)
            within = pl.ds(pl.multiple_of(sum_at + r * tile, tile), tile)
            if not outs and (add or c > 0):
                sum_ref[within, :] += term
            elif not outs:
                sum_ref[within, :] = term
            else:
                term += acc_ref[within, :]
                ends = [sum(n for n, _ in outs[: i + 1]) for i in range(len(outs))]
                for t in range(rows // tile):

                    @pl.when(r == t)
                    def _(t=t):
                        for (n, dtype), end, ref in zip(outs, ends, out_refs):
                            if t * tile < end <= (t + 1) * tile:
                                ref[...] = term[end - n - t * tile : end - t * tile].astype(dtype)


def net(xs, pieces, depths, tile, limit, total, total_at, add, outs=()):
    rows, width = sum(a.shape[0] for a in xs), xs[0].shape[1]
    fresh = isinstance(total, int)
    hidden = sum(depths)
    assert not outs or len(depths) == 1
    operands = list(xs) + [p[0] for p in pieces] + ([] if fresh else [total])
    shapes = outs or [(total if fresh else total.shape[0], F32)]
    return pl.pallas_call(
        functools.partial(net_kernel, len(xs), tuple(p[1:] for p in pieces), tuple(depths), total_at, add, tuple(outs), tile),
        out_shape=[pltpu.VMEM((n, width), d) for n, d in shapes],
        in_specs=whole(len(operands)),
        out_specs=whole(len(shapes)),
        input_output_aliases={} if fresh or outs else {len(operands) - 1: 0},
        scratch_shapes=[
            pltpu.VMEM((rows, width), BF16),
            pltpu.VMEM((2 * hidden, width), BF16),
            pltpu.VMEM((hidden, width), BF16),
            pltpu.SemaphoreType.DMA((len(xs),)),
            pltpu.SemaphoreType.DMA((len(pieces) * 6,)),
        ],
        compiler_params=params(limit),
        cost_estimate=pl.CostEstimate(
            flops=rows * width * hidden * 6, bytes_accessed=rows * width * 8 + hidden * width * 6, transcendentals=rows * hidden
        ),
        name="networks",
    )(*(near(a) for a in operands))


def per_device(tokens, routes, gate_num, student_gate, student_up, student_down, teacher_gate, teacher_up, teacher_down):
    here = lax.axis_index("expert").astype(jnp.int32).reshape(1)
    routes, gate_num = routes.T, gate_num.T
    width = tokens.shape[1]
    units = student_gate.shape[2]
    block = EXPERTS * CAP
    half = block // 2
    mib = 1024 * 1024

    student, rows = pack((student_gate[0], student_up[0], student_down[0]), routes, tokens)
    (teacher,) = pack((teacher_gate[0], teacher_up[0], teacher_down[0]))
    prev_student = send(student, ring(1, True))
    next_teacher = send(teacher, ring(-1, True))
    rows, teacher = barrier(rows, teacher)
    rows = rows.reshape(EXPERTS, CAP, width)
    rows = lax.all_to_all(rows, "expert", split_axis=0, concat_axis=0, tiled=True).reshape(block, width)

    prev_rows = send(rows, ring(1, False))
    next_rows = send(rows, ring(-1, False))
    first = [(student, False, 0, units), (teacher, True, 0, units), (prev_student, False, 0, units), (next_teacher, True, 0, units)]
    (total,) = net([rows], first, [512, 768], block, 28 * mib, 4 * block, 3 * block, False)

    total, prev_student, next_teacher, prev_rows, next_rows = barrier(total, prev_student, next_teacher, prev_rows, next_rows)
    far_student = send(prev_student, ring(1, True))
    far_teacher = send(next_teacher, ring(-1, True))
    far_a = send(prev_rows[:half], ring(1, False))
    far_b = send(next_rows[half:], ring(-1, False))
    first = [(student, False, 0, units), (teacher, True, 0, units), (prev_student, False, 0, units), (next_teacher, True, 0, units)]
    near_xs = [next_rows, prev_rows]
    (total,) = net(near_xs, first, [512, 768], block, 28 * mib, total, block, False)

    total, far_a, far_b, student, teacher = barrier(total, far_a, far_b, student, teacher)
    prev_teacher = send(teacher, ring(1, True))
    next_student = send(student, ring(-1, True))
    first[:2] = [(student, False, 0, units), (teacher, True, 0, units)]
    far_xs = [far_a, far_b]
    (total,) = net(far_xs, first, [512, 768], block, 28 * mib, total, 0, False)
    high, low = shares(routes, gate_num)

    second = [(far_student, False, 0, units), (far_teacher, True, 0, units)]
    last = [(prev_teacher, True, 0, units), (next_student, False, 0, units)]
    (total,) = net(far_xs + near_xs + [rows], second, [640], 2 * block, 24 * mib, total, 0, True)
    (far_sum,) = net(far_xs, last, [640], block, 16 * mib, total, 0, True, [(block, BF16)])
    total, far_sum = barrier(total, far_sum)
    far_sum = send(far_sum, ring(2, False))
    to_next, to_prev = net(near_xs, last, [640], block, 16 * mib, total, block, True, [(block, BF16), (block, BF16)])
    prev_sum = send(to_next, ring(1, False))
    next_sum = send(to_prev, ring(-1, False))
    total, far_sum, _, _ = barrier(total, far_sum, to_next, to_prev)
    (own,) = net([rows], last, [640], block, 16 * mib, total, 3 * block, True, [(block, F32)])
    blocks = sum_rows(here, own, far_sum, prev_sum, next_sum)
    return combine(here, high, low, [blocks[0]] + [send(blocks[d], hop(d, True)) for d in range(1, EXPERTS)])


def solution(mesh):
    in_specs = (
        P(("expert", "shard"), None),
        P(("expert", "shard"), None),
        P(("expert", "shard"), None),
        P("expert", None, "shard"),
        P("expert", None, "shard"),
        P("expert", "shard", None),
        P("expert", None, "shard"),
        P("expert", None, "shard"),
        P("expert", "shard", None),
    )
    out_specs = P(("expert", "shard"), None)
    return jax.shard_map(
        per_device, mesh=mesh, in_specs=in_specs, out_specs=out_specs, check_vma=False
    )
```

```python
import functools

import jax
import jax.numpy as jnp
from jax import lax
from jax.experimental import pallas as pl
from jax.experimental.pallas import tpu as pltpu
from jax.sharding import PartitionSpec as P

AXES = ("expert", "shard")
BF16 = jnp.bfloat16
F32 = jnp.float32
CAP = 48
EXPERTS = 8
VMEM_LIMIT = 16 * 1024 * 1024


def dev(z, c, y, x):
    return ((z % 4 * 2 + c % 2) * 4 + y % 4) * 4 + x % 4


COORDS = [(z, c, y, x) for z in range(4) for c in range(2) for y in range(4) for x in range(4)]


def ring(step, weights):
    return [
        (dev(z, c, y, x), dev(z, c, y, x + step) if (c == 0) == weights else dev(z, c, y + step, x))
        for z, c, y, x in COORDS
    ]


def cross(step):
    return [(dev(z, c, y, x), dev(z, 1 - c, y + step, x) if c == 0 else dev(z, 1 - c, y, x + step)) for z, c, y, x in COORDS]


def along_z(step):
    return [(dev(z, c, y, x), dev(z + step, c, y, x)) for z, c, y, x in COORDS]


def send(value, pairs):
    return lax.ppermute(value, AXES, pairs)


def barrier(*values):
    return lax.optimization_barrier(values)


def whole(count, space=pltpu.VMEM):
    return [pl.BlockSpec(memory_space=space)] * count


def params(limit=VMEM_LIMIT):
    return pltpu.CompilerParams(vmem_limit_bytes=limit)


def near(value):
    return pltpu.with_memory_space_constraint(value, pltpu.VMEM)


def places(routes_ref):
    tokens = routes_ref.shape[1]
    first, second = routes_ref[0:1, :], routes_ref[1:2, :]
    expert = lax.broadcasted_iota(jnp.int32, (16, tokens), 0)
    named = ((expert == first).astype(F32) + (expert == second).astype(F32)).astype(BF16)
    before = lax.broadcasted_iota(jnp.int32, (tokens, tokens), 0) < lax.broadcasted_iota(jnp.int32, (tokens, tokens), 1)
    earlier = jnp.dot(named, before.astype(F32).astype(BF16), preferred_element_type=F32)
    found = []
    for ids, extra in ((first, 0), (second, (first == second).astype(jnp.int32))):
        slot = jnp.sum(jnp.where(expert == ids, earlier, 0.0), axis=0, keepdims=True).astype(jnp.int32) + extra
        found.append(ids * CAP + slot)
    return found


def pack_kernel(n_rest, *refs):
    weight_refs, rest, packed_ref = refs[:3], refs[3 : 3 + n_rest], refs[3 + n_rest]
    sems = refs[-1]
    units = weight_refs[0].shape[0]
    ins = [
        pltpu.make_async_copy(ref, packed_ref.at[pl.ds(i * units, units)], sems.at[i]) for i, ref in enumerate(weight_refs)
    ]
    for copy in ins:
        copy.start()
    if rest:
        routes_ref, tokens_ref = rest
        first, second = places(routes_ref)
        slots = lax.broadcasted_iota(jnp.int32, (EXPERTS * CAP, tokens_ref.shape[0]), 0)
        chosen = ((slots == first) | (slots == second)).astype(F32).astype(BF16)
        refs[4 + n_rest][...] = jnp.dot(chosen, tokens_ref[...], preferred_element_type=F32).astype(BF16)
    for copy in ins:
        copy.wait()


def pack(weights, *rest):
    gate, up, down = weights
    units, width = down.shape
    rows = [pltpu.VMEM((EXPERTS * CAP, width), BF16)] if rest else []
    return pl.pallas_call(
        functools.partial(pack_kernel, len(rest)),
        out_shape=[pltpu.VMEM((3 * units, width), BF16)] + rows,
        in_specs=whole(3, pltpu.HBM) + whole(len(rest)),
        out_specs=whole(1 + len(rows)),
        scratch_shapes=[pltpu.SemaphoreType.DMA((3,))],
        compiler_params=params(58 * 1024 * 1024 if rest else VMEM_LIMIT),
        cost_estimate=pl.CostEstimate(flops=100_000_000, bytes_accessed=4_000_000, transcendentals=0),
        name="pack_weights",
    )(gate.T, up.T, down, *rest)


def split_kernel(cut, *refs):
    n = (len(refs) - 1) // 3
    sems, copies = refs[-1], []
    for i in range(n):
        units = refs[i].shape[0] // 3
        for ref, first, count in ((refs[n + 2 * i], 0, cut), (refs[n + 2 * i + 1], cut, units - cut)):
            for k in range(3):
                pair = refs[i].at[pl.ds(k * units + first, count)], ref.at[pl.ds(k * count, count)]
                copies.append(pltpu.make_async_copy(*pair, sems.at[len(copies)]))
    for copy in copies:
        copy.start()
    for copy in copies:
        copy.wait()


def split(cut, *packed):
    shapes = [pltpu.VMEM((3 * n, p.shape[1]), BF16) for p in packed for n in (cut, p.shape[0] // 3 - cut)]
    return pl.pallas_call(
        functools.partial(split_kernel, cut),
        out_shape=shapes,
        in_specs=whole(len(packed)),
        out_specs=whole(len(shapes)),
        scratch_shapes=[pltpu.SemaphoreType.DMA((6 * len(packed),))],
        compiler_params=params(),
        cost_estimate=pl.CostEstimate(flops=0, bytes_accessed=6_000_000, transcendentals=0),
        name="split_weights",
    )(*(near(p) for p in packed))


def shares_kernel(routes_ref, gates_ref, high_ref, low_ref):
    first, second = places(routes_ref)
    gates = gates_ref[...].astype(F32)
    share = gates / jnp.sum(gates, axis=0, keepdims=True)
    slots = lax.broadcasted_iota(jnp.int32, (EXPERTS * CAP, routes_ref.shape[1]), 0)
    weight = jnp.where(slots == first, share[0:1], 0.0) + jnp.where(slots == second, share[1:2], 0.0)
    weight = weight.T
    high = weight.astype(BF16)
    high_ref[...] = high
    low_ref[...] = (weight - high.astype(F32)).astype(BF16)


def shares(routes, gates):
    tokens = routes.shape[1]
    return pl.pallas_call(
        shares_kernel,
        out_shape=[jax.ShapeDtypeStruct((tokens, EXPERTS * CAP), BF16)] * 2,
        in_specs=whole(2),
        out_specs=whole(2),
        compiler_params=params(),
        cost_estimate=pl.CostEstimate(flops=10_000_000, bytes_accessed=1_000_000, transcendentals=0),
        name="gate_shares",
    )(routes, gates)


def block_of(place):
    return pl.ds(pl.multiple_of(place * CAP, CAP), CAP)


def halves_kernel(here_ref, own_ref, far_ref, keep_ref, give_ref):
    core = here_ref[0] & 1
    for z in range(EXPERTS // 2):
        to = slice(z * CAP, (z + 1) * CAP)
        at = block_of(2 * z + core)
        keep_ref[to] = own_ref[at, :] + far_ref[at, :].astype(F32)
        at = block_of(2 * z + 1 - core)
        give_ref[to] = (own_ref[at, :] + far_ref[at, :].astype(F32)).astype(BF16)


def halves(here, own, far_part):
    rows, width = own.shape
    return pl.pallas_call(
        halves_kernel,
        out_shape=[pltpu.VMEM((rows // 2, width), F32), pltpu.VMEM((rows // 2, width), BF16)],
        in_specs=whole(1, pltpu.SMEM) + whole(2),
        out_specs=whole(2),
        compiler_params=params(),
        cost_estimate=pl.CostEstimate(flops=1_000_000, bytes_accessed=3_000_000, transcendentals=0),
        name="halve_rows",
    )(here, near(own), near(far_part))


def sum_kernel(here_ref, keep_ref, prev_ref, next_ref, given_ref, prev_other_ref, next_other_ref, *out_refs):
    z = here_ref[0] >> 1
    for step, out_ref in enumerate(out_refs):
        at = block_of((z + step) & 3)
        mine = keep_ref[at, :] + prev_ref[at, :].astype(F32) + next_ref[at, :].astype(F32)
        other = given_ref[at, :].astype(F32) + prev_other_ref[at, :].astype(F32) + next_other_ref[at, :].astype(F32)
        out_ref[:CAP] = mine.astype(BF16)
        out_ref[CAP:] = other.astype(BF16)


def sum_rows(here, *parts):
    steps, width = EXPERTS // 2, parts[0].shape[1]
    return pl.pallas_call(
        sum_kernel,
        out_shape=[pltpu.VMEM((2 * CAP, width), BF16)] * steps,
        in_specs=whole(1, pltpu.SMEM) + whole(len(parts)),
        out_specs=whole(steps),
        compiler_params=params(),
        cost_estimate=pl.CostEstimate(flops=1_000_000, bytes_accessed=4_000_000, transcendentals=0),
        name="sum_rows",
    )(here, *(near(p) for p in parts))


def combine_kernel(here_ref, high_ref, low_ref, *refs):
    *block_refs, out_ref, held = refs
    z, core = here_ref[0] >> 1, here_ref[0] & 1
    for step, ref in enumerate(block_refs):
        chip = 2 * ((z - step) & 3)
        held[block_of(chip + core), :] = ref[:CAP]
        held[block_of(chip + 1 - core), :] = ref[CAP:]
    rows = held[...]
    total = jnp.dot(high_ref[...], rows, preferred_element_type=F32)
    total += jnp.dot(low_ref[...], rows, preferred_element_type=F32)
    out_ref[...] = total.astype(BF16)


def combine(here, high, low, blocks):
    tokens, width = high.shape[0], blocks[0].shape[1]
    return pl.pallas_call(
        combine_kernel,
        out_shape=jax.ShapeDtypeStruct((tokens, width), BF16),
        in_specs=whole(1, pltpu.SMEM) + whole(2 + len(blocks)),
        out_specs=pl.BlockSpec(memory_space=pltpu.VMEM),
        scratch_shapes=[pltpu.VMEM((EXPERTS * CAP, width), BF16)],
        compiler_params=params(),
        cost_estimate=pl.CostEstimate(flops=200_000_000, bytes_accessed=1_000_000, transcendentals=0),
        name="combine_rows",
    )(here, near(high), near(low), *(near(b) for b in blocks))


def net_kernel(n_x, pieces, depths, sum_at, add, outs, tile, *refs):
    x_refs, refs = refs[:n_x], refs[n_x:]
    piece_refs, refs = refs[: len(pieces)], refs[len(pieces) :]
    n_sums = len(refs) - max(len(outs), 1) - 5
    if n_sums:
        acc_ref, refs = refs[0], refs[1:]
    if outs:
        out_refs, refs = refs[: len(outs)], refs[len(outs) :]
    else:
        sum_ref, refs = refs[0], refs[1:]
    x, gate_up, down, x_sem, w_sem = refs
    rows, width = x.shape
    starts = [sum(depths[:c]) for c in range(len(depths))]

    wide_pairs, down_pairs, negative = ([[] for _ in depths] for _ in range(3))
    at = 0
    for ref, (teacher, first, count) in zip(piece_refs, pieces):
        units, done = ref.shape[0] // 3, 0
        while done < count:
            chunk = max(c for c in range(len(depths)) if starts[c] <= at)
            n = min(count - done, starts[chunk] + depths[chunk] - at)
            inside = at - starts[chunk]
            for k in range(2):
                to = 2 * starts[chunk] + k * depths[chunk] + inside
                wide_pairs[chunk].append((ref.at[pl.ds(k * units + first + done, n)], gate_up.at[pl.ds(to, n)]))
            down_pairs[chunk].append((ref.at[pl.ds(2 * units + first + done, n)], down.at[pl.ds(at, n)]))
            if teacher:
                negative[chunk].append((at, n))
            at += n
            done += n
    used = at

    def copies_of(pairs, base):
        return [pltpu.make_async_copy(a, b, w_sem.at[base + i]) for i, (a, b) in enumerate(pairs)]

    wide_copies, down_copies, base = [], [], 0
    for c in range(len(depths)):
        wide_copies.append(copies_of(wide_pairs[c], base))
        base += len(wide_pairs[c])
        down_copies.append(copies_of(down_pairs[c], base))
        base += len(down_pairs[c])

    x_copies, at = [], 0
    for i, ref in enumerate(x_refs):
        x_copies.append(pltpu.make_async_copy(ref, x.at[pl.ds(at, ref.shape[0])], x_sem.at[i]))
        at += ref.shape[0]

    for copy in x_copies:
        copy.start()
    for c in range(len(depths)):
        for copy in wide_copies[c] + down_copies[c]:
            copy.start()
    if used < sum(depths):
        c = len(depths) - 1
        empty = sum(depths) - used
        zeros = jnp.zeros((empty, width), BF16)
        for k in range(2):
            end = 2 * starts[c] + (k + 1) * depths[c]
            gate_up[end - empty : end, :] = zeros
        down[used:, :] = zeros
    for copy in x_copies:
        copy.wait()

    for c, depth in enumerate(depths):
        for copy in wide_copies[c]:
            copy.wait()

        @pl.loop(0, rows // tile)
        def _(r, c=c, depth=depth):
            at = pl.ds(pl.multiple_of(r * tile, tile), tile)
            low = 2 * starts[c]
            rows_in = x[at, :]
            turned = (((1,), (1,)), ((), ()))
            gate = lax.dot_general(rows_in, gate_up[low : low + depth], turned, preferred_element_type=F32)
            up = lax.dot_general(rows_in, gate_up[low + depth : low + 2 * depth], turned, preferred_element_type=F32)
            hidden = (gate / (1.0 + jnp.exp(-gate)) * up).astype(BF16)

            @pl.when(r == 0)
            def _():
                for copy in down_copies[c]:
                    copy.wait()
                for first, n in negative[c]:
                    down[first : first + n, :] = -down[first : first + n, :]

            term = jnp.dot(hidden, down[starts[c] : starts[c] + depth], preferred_element_type=F32)
            within = pl.ds(pl.multiple_of(sum_at + r * tile, tile), tile)
            if not outs and (add or c > 0):
                sum_ref[within, :] += term
            elif not outs:
                sum_ref[within, :] = term
            else:
                term += acc_ref[within, :]
                ends = [sum(n for n, _ in outs[: i + 1]) for i in range(len(outs))]
                for t in range(rows // tile):

                    @pl.when(r == t)
                    def _(t=t):
                        for (n, dtype), end, ref in zip(outs, ends, out_refs):
                            if t * tile < end <= (t + 1) * tile:
                                ref[...] = term[end - n - t * tile : end - t * tile].astype(dtype)


def last_kernel(teacher, sum_at, halved, *refs):
    if halved:
        here_ref, *refs, held = refs
        refs, out_refs = refs[:-4], refs[-4:]
        *refs, sum_ref = refs
    else:
        *refs, sum_ref, out_ref = refs
    x_refs, piece_refs = refs[: -len(teacher)], refs[-len(teacher) :]
    x = x_refs[0][...] if len(x_refs) == 1 else jnp.concatenate([r[...] for r in x_refs], axis=0)
    total = sum_ref[sum_at : sum_at + x.shape[0], :]
    for ref, negative in zip(piece_refs, teacher):
        units = ref.shape[0] // 3
        wide = lax.dot_general(x, ref[: 2 * units], (((1,), (1,)), ((), ())), preferred_element_type=F32)
        gate, up = wide[:, :units], wide[:, units:]
        hidden = (gate / (1.0 + jnp.exp(-gate)) * up).astype(BF16)
        term = jnp.dot(hidden, ref[2 * units :], preferred_element_type=F32)
        total = total - term if negative else total + term
    if not halved:
        out_ref[...] = total.astype(out_ref.dtype)
        return
    held[...] = total
    for i, out_ref in enumerate(out_refs):
        for z in range(EXPERTS // 2):
            place = EXPERTS * (i // 2) + 2 * z + ((here_ref[0] + i) & 1)
            out_ref[z * CAP : (z + 1) * CAP] = held[block_of(place), :].astype(out_ref.dtype)


def last_net(xs, pieces, total, total_at, dtype, here=None):
    rows, width = sum(a.shape[0] for a in xs), xs[0].shape[1]
    halved = here is not None
    hidden = sum(p.shape[0] // 3 for p, _ in pieces)
    operands = list(xs) + [p for p, _ in pieces] + [total]
    return pl.pallas_call(
        functools.partial(last_kernel, tuple(t for _, t in pieces), total_at, halved),
        out_shape=[pltpu.VMEM((rows // 4, width), dtype)] * 4 if halved else pltpu.VMEM((rows, width), dtype),
        in_specs=(whole(1, pltpu.SMEM) if halved else []) + whole(len(operands)),
        out_specs=whole(4) if halved else whole(1)[0],
        scratch_shapes=[pltpu.VMEM((rows, width), F32)] if halved else [],
        compiler_params=params(),
        cost_estimate=pl.CostEstimate(
            flops=rows * width * hidden * 6, bytes_accessed=rows * width * 8 + hidden * width * 6, transcendentals=rows * hidden
        ),
        name="networks_last",
    )(*([here] if halved else []), *(near(a) for a in operands))


def net(xs, pieces, depths, tile, limit, total, total_at, add, outs=()):
    rows, width = sum(a.shape[0] for a in xs), xs[0].shape[1]
    fresh = isinstance(total, int)
    hidden = sum(depths)
    assert not outs or len(depths) == 1
    operands = list(xs) + [p[0] for p in pieces] + ([] if fresh else [total])
    shapes = outs or [(total if fresh else total.shape[0], F32)]
    return pl.pallas_call(
        functools.partial(net_kernel, len(xs), tuple(p[1:] for p in pieces), tuple(depths), total_at, add, tuple(outs), tile),
        out_shape=[pltpu.VMEM((n, width), d) for n, d in shapes],
        in_specs=whole(len(operands)),
        out_specs=whole(len(shapes)),
        input_output_aliases={} if fresh or outs else {len(operands) - 1: 0},
        scratch_shapes=[
            pltpu.VMEM((rows, width), BF16),
            pltpu.VMEM((2 * hidden, width), BF16),
            pltpu.VMEM((hidden, width), BF16),
            pltpu.SemaphoreType.DMA((len(xs),)),
            pltpu.SemaphoreType.DMA((len(pieces) * 6,)),
        ],
        compiler_params=params(limit),
        cost_estimate=pl.CostEstimate(
            flops=rows * width * hidden * 6, bytes_accessed=rows * width * 8 + hidden * width * 6, transcendentals=rows * hidden
        ),
        name="networks",
    )(*(near(a) for a in operands))


def per_device(tokens, routes, gate_num, student_gate, student_up, student_down, teacher_gate, teacher_up, teacher_down):
    here = lax.axis_index("expert").astype(jnp.int32).reshape(1)
    routes, gate_num = routes.T, gate_num.T
    width = tokens.shape[1]
    units = student_gate.shape[2]
    block = EXPERTS * CAP
    half = block // 2
    mib = 1024 * 1024
    cut = units - 128

    student, rows = pack((student_gate[0], student_up[0], student_down[0]), routes, tokens)
    (teacher,) = pack((teacher_gate[0], teacher_up[0], teacher_down[0]))
    prev_student = send(student, ring(1, True))
    next_teacher = send(teacher, ring(-1, True))
    rows, teacher = barrier(rows, teacher)
    rows = rows.reshape(EXPERTS, CAP, width)
    rows = lax.all_to_all(rows, "expert", split_axis=0, concat_axis=0, tiled=True).reshape(block, width)

    prev_rows = send(rows, ring(1, False))
    next_rows = send(rows, ring(-1, False))
    first = [(student, False, 0, units), (teacher, True, 0, units), (prev_student, False, 0, units), (next_teacher, True, 0, units)]
    (total,) = net([rows], first, [512, 768], block, 28 * mib, 4 * block, 3 * block, False)

    parts = split(cut, barrier(student, total)[0], teacher)
    total, prev_student, next_teacher, prev_rows, next_rows, *parts = barrier(
        total, prev_student, next_teacher, prev_rows, next_rows, *parts
    )
    far_student = send(prev_student, ring(1, True))
    far_teacher = send(next_teacher, ring(-1, True))
    far_a = send(prev_rows[:half], ring(1, False))
    far_b = send(next_rows[half:], ring(-1, False))
    first = [(student, False, 0, units), (teacher, True, 0, units), (prev_student, False, 0, units), (next_teacher, True, 0, units)]
    near_xs = [next_rows, prev_rows]
    (total,) = net(near_xs, first, [512, 768], 2 * block, 32 * mib, total, block, False)

    total, far_a, far_b, *parts = barrier(total, far_a, far_b, *parts)
    student_a, student_b, teacher_a, teacher_b = parts
    prev_teacher_a = send(teacher_a, ring(1, True))
    next_student_a = send(student_a, ring(-1, True))
    far_xs = [far_a, far_b]
    (total,) = net(far_xs, first, [512, 768], block, 28 * mib, total, 0, False)
    high, low = shares(routes, gate_num)

    total, far_student, far_teacher, student_b, teacher_b = barrier(total, far_student, far_teacher, student_b, teacher_b)
    room = 512 - units
    second = [(far_student, False, 0, units), (far_teacher, True, 0, room)]
    third = [(far_teacher, True, room, units - room), (prev_teacher_a, True, 0, cut), (next_student_a, False, 0, cut)]
    last = [(send(teacher_b, ring(1, True)), True), (send(student_b, ring(-1, True)), False)]
    (total,) = net(far_xs + near_xs + [rows], second, [512], 2 * block, 24 * mib, total, 0, True)
    (total,) = net(far_xs + near_xs + [rows], third, [512], 2 * block, 24 * mib, total, 0, True)
    far_sum = last_net(far_xs, last, total, 0, BF16)
    total, far_sum = barrier(total, far_sum)
    far_sum = send(far_sum, ring(2, False))
    next_same, next_other, prev_same, prev_other = last_net(near_xs, last, total, block, BF16, here)
    total, _ = barrier(total, next_same)
    prev_part, prev_cross = send(next_same, ring(1, False)), send(next_other, cross(1))
    next_part, next_cross = send(prev_same, ring(-1, False)), send(prev_other, cross(-1))
    own = last_net([rows], last, total, 3 * block, F32)
    keep, give = halves(here, own, far_sum)
    given = send(give, cross(0))
    blocks = sum_rows(here, keep, prev_part, next_part, given, prev_cross, next_cross)
    return combine(here, high, low, [blocks[0]] + [send(blocks[step], along_z(step)) for step in range(1, EXPERTS // 2)])


def solution(mesh):
    in_specs = (
        P(("expert", "shard"), None),
        P(("expert", "shard"), None),
        P(("expert", "shard"), None),
        P("expert", None, "shard"),
        P("expert", None, "shard"),
        P("expert", "shard", None),
        P("expert", None, "shard"),
        P("expert", None, "shard"),
        P("expert", "shard", None),
    )
    out_specs = P(("expert", "shard"), None)
    return jax.shard_map(
        per_device, mesh=mesh, in_specs=in_specs, out_specs=out_specs, check_vma=False
    )
```

```python
import functools

import jax
import jax.numpy as jnp
from jax import lax
from jax.experimental import pallas as pl
from jax.experimental.pallas import tpu as pltpu
from jax.sharding import PartitionSpec as P

AXES = ("expert", "shard")
BF16 = jnp.bfloat16
F32 = jnp.float32
CAP = 48
EXPERTS = 8
VMEM_LIMIT = 16 * 1024 * 1024


def dev(z, c, y, x):
    return ((z % 4 * 2 + c % 2) * 4 + y % 4) * 4 + x % 4


COORDS = [(z, c, y, x) for z in range(4) for c in range(2) for y in range(4) for x in range(4)]


def ring(step, weights):
    return [
        (dev(z, c, y, x), dev(z, c, y, x + step) if (c == 0) == weights else dev(z, c, y + step, x))
        for z, c, y, x in COORDS
    ]


def cross(step):
    return [(dev(z, c, y, x), dev(z, 1 - c, y + step, x) if c == 0 else dev(z, 1 - c, y, x + step)) for z, c, y, x in COORDS]


def along_z(step):
    return [(dev(z, c, y, x), dev(z + step, c, y, x)) for z, c, y, x in COORDS]


def send(value, pairs):
    return lax.ppermute(value, AXES, pairs)


def barrier(*values):
    return lax.optimization_barrier(values)


def whole(count, space=pltpu.VMEM):
    return [pl.BlockSpec(memory_space=space)] * count


def params(limit=VMEM_LIMIT):
    return pltpu.CompilerParams(vmem_limit_bytes=limit)


def near(value):
    return pltpu.with_memory_space_constraint(value, pltpu.VMEM)


def places(routes_ref):
    tokens = routes_ref.shape[1]
    first, second = routes_ref[0:1, :], routes_ref[1:2, :]
    expert = lax.broadcasted_iota(jnp.int32, (16, tokens), 0)
    named = ((expert == first).astype(F32) + (expert == second).astype(F32)).astype(BF16)
    before = lax.broadcasted_iota(jnp.int32, (tokens, tokens), 0) < lax.broadcasted_iota(jnp.int32, (tokens, tokens), 1)
    earlier = jnp.dot(named, before.astype(F32).astype(BF16), preferred_element_type=F32)
    found = []
    for ids, extra in ((first, 0), (second, (first == second).astype(jnp.int32))):
        slot = jnp.sum(jnp.where(expert == ids, earlier, 0.0), axis=0, keepdims=True).astype(jnp.int32) + extra
        found.append(ids * CAP + slot)
    return found


def pack_kernel(n_rest, *refs):
    weight_refs, rest, packed_ref = refs[:3], refs[3 : 3 + n_rest], refs[3 + n_rest]
    sems = refs[-1]
    units = weight_refs[0].shape[0]
    ins = [
        pltpu.make_async_copy(ref, packed_ref.at[pl.ds(i * units, units)], sems.at[i]) for i, ref in enumerate(weight_refs)
    ]
    for copy in ins:
        copy.start()
    if rest:
        routes_ref, tokens_ref = rest
        first, second = places(routes_ref)
        slots = lax.broadcasted_iota(jnp.int32, (EXPERTS * CAP, tokens_ref.shape[0]), 0)
        chosen = ((slots == first) | (slots == second)).astype(F32).astype(BF16)
        refs[4 + n_rest][...] = jnp.dot(chosen, tokens_ref[...], preferred_element_type=F32).astype(BF16)
    for copy in ins:
        copy.wait()


def pack(weights, *rest):
    gate, up, down = weights
    units, width = down.shape
    rows = [pltpu.VMEM((EXPERTS * CAP, width), BF16)] if rest else []
    return pl.pallas_call(
        functools.partial(pack_kernel, len(rest)),
        out_shape=[pltpu.VMEM((3 * units, width), BF16)] + rows,
        in_specs=whole(3, pltpu.HBM) + whole(len(rest)),
        out_specs=whole(1 + len(rows)),
        scratch_shapes=[pltpu.SemaphoreType.DMA((3,))],
        compiler_params=params(58 * 1024 * 1024 if rest else VMEM_LIMIT),
        cost_estimate=pl.CostEstimate(flops=100_000_000, bytes_accessed=4_000_000, transcendentals=0),
        name="pack_weights",
    )(gate.T, up.T, down, *rest)


def split_kernel(cut, *refs):
    n = len(refs) // 3
    for i in range(n):
        units = refs[i].shape[0] // 3
        for ref, first, count in ((refs[n + 2 * i], 0, cut), (refs[n + 2 * i + 1], cut, units - cut)):
            for k in range(3):
                ref[k * count : (k + 1) * count] = refs[i][k * units + first : k * units + first + count]


def split(cut, *packed):
    shapes = [pltpu.VMEM((3 * n, p.shape[1]), BF16) for p in packed for n in (cut, p.shape[0] // 3 - cut)]
    return pl.pallas_call(
        functools.partial(split_kernel, cut),
        out_shape=shapes,
        in_specs=whole(len(packed)),
        out_specs=whole(len(shapes)),
        compiler_params=params(),
        cost_estimate=pl.CostEstimate(flops=0, bytes_accessed=6_000_000, transcendentals=0),
        name="split_weights",
    )(*(near(p) for p in packed))


def shares_kernel(routes_ref, gates_ref, high_ref, low_ref):
    first, second = places(routes_ref)
    gates = gates_ref[...].astype(F32)
    share = gates / jnp.sum(gates, axis=0, keepdims=True)
    slots = lax.broadcasted_iota(jnp.int32, (EXPERTS * CAP, routes_ref.shape[1]), 0)
    weight = jnp.where(slots == first, share[0:1], 0.0) + jnp.where(slots == second, share[1:2], 0.0)
    weight = weight.T
    high = weight.astype(BF16)
    high_ref[...] = high
    low_ref[...] = (weight - high.astype(F32)).astype(BF16)


def shares(routes, gates):
    tokens = routes.shape[1]
    return pl.pallas_call(
        shares_kernel,
        out_shape=[jax.ShapeDtypeStruct((tokens, EXPERTS * CAP), BF16)] * 2,
        in_specs=whole(2),
        out_specs=whole(2),
        compiler_params=params(),
        cost_estimate=pl.CostEstimate(flops=10_000_000, bytes_accessed=1_000_000, transcendentals=0),
        name="gate_shares",
    )(routes, gates)


def block_of(place):
    return pl.ds(pl.multiple_of(place * CAP, CAP), CAP)


def halves_kernel(here_ref, own_ref, far_ref, keep_ref, give_ref):
    core = here_ref[0] & 1
    for z in range(EXPERTS // 2):
        to = slice(z * CAP, (z + 1) * CAP)
        at = block_of(2 * z + core)
        keep_ref[to] = own_ref[at, :] + far_ref[at, :].astype(F32)
        at = block_of(2 * z + 1 - core)
        give_ref[to] = (own_ref[at, :] + far_ref[at, :].astype(F32)).astype(BF16)


def halves(here, own, far_part):
    rows, width = own.shape
    return pl.pallas_call(
        halves_kernel,
        out_shape=[pltpu.VMEM((rows // 2, width), F32), pltpu.VMEM((rows // 2, width), BF16)],
        in_specs=whole(1, pltpu.SMEM) + whole(2),
        out_specs=whole(2),
        compiler_params=params(),
        cost_estimate=pl.CostEstimate(flops=1_000_000, bytes_accessed=3_000_000, transcendentals=0),
        name="halve_rows",
    )(here, near(own), near(far_part))


def sum_kernel(here_ref, keep_ref, prev_ref, next_ref, given_ref, prev_other_ref, next_other_ref, *out_refs):
    z = here_ref[0] >> 1
    for step, out_ref in enumerate(out_refs):
        at = block_of((z + step) & 3)
        mine = keep_ref[at, :] + prev_ref[at, :].astype(F32) + next_ref[at, :].astype(F32)
        other = given_ref[at, :].astype(F32) + prev_other_ref[at, :].astype(F32) + next_other_ref[at, :].astype(F32)
        out_ref[:CAP] = mine.astype(BF16)
        out_ref[CAP:] = other.astype(BF16)


def sum_rows(here, *parts):
    steps, width = EXPERTS // 2, parts[0].shape[1]
    return pl.pallas_call(
        sum_kernel,
        out_shape=[pltpu.VMEM((2 * CAP, width), BF16)] * steps,
        in_specs=whole(1, pltpu.SMEM) + whole(len(parts)),
        out_specs=whole(steps),
        compiler_params=params(),
        cost_estimate=pl.CostEstimate(flops=1_000_000, bytes_accessed=4_000_000, transcendentals=0),
        name="sum_rows",
    )(here, *(near(p) for p in parts))


def combine_kernel(here_ref, high_ref, low_ref, *refs):
    *block_refs, out_ref, held = refs
    z, core = here_ref[0] >> 1, here_ref[0] & 1
    for step, ref in enumerate(block_refs):
        chip = 2 * ((z - step) & 3)
        held[block_of(chip + core), :] = ref[:CAP]
        held[block_of(chip + 1 - core), :] = ref[CAP:]
    rows = held[...]
    total = jnp.dot(high_ref[...], rows, preferred_element_type=F32)
    total += jnp.dot(low_ref[...], rows, preferred_element_type=F32)
    out_ref[...] = total.astype(BF16)


def combine(here, high, low, blocks):
    tokens, width = high.shape[0], blocks[0].shape[1]
    return pl.pallas_call(
        combine_kernel,
        out_shape=jax.ShapeDtypeStruct((tokens, width), BF16),
        in_specs=whole(1, pltpu.SMEM) + whole(2 + len(blocks)),
        out_specs=pl.BlockSpec(memory_space=pltpu.VMEM),
        scratch_shapes=[pltpu.VMEM((EXPERTS * CAP, width), BF16)],
        compiler_params=params(),
        cost_estimate=pl.CostEstimate(flops=200_000_000, bytes_accessed=1_000_000, transcendentals=0),
        name="combine_rows",
    )(here, near(high), near(low), *(near(b) for b in blocks))


def net_kernel(n_x, pieces, depths, sum_at, add, outs, tile, *refs):
    x_refs, refs = refs[:n_x], refs[n_x:]
    piece_refs, refs = refs[: len(pieces)], refs[len(pieces) :]
    n_sums = len(refs) - max(len(outs), 1) - 3
    if n_sums:
        acc_ref, refs = refs[0], refs[1:]
    if outs:
        out_refs, refs = refs[: len(outs)], refs[len(outs) :]
    else:
        sum_ref, refs = refs[0], refs[1:]
    x, gate_up, down = refs
    rows, width = x.shape
    starts = [sum(depths[:c]) for c in range(len(depths))]

    at = 0
    for ref in x_refs:
        x[at : at + ref.shape[0], :] = ref[...]
        at += ref.shape[0]

    spans, at = [[] for _ in depths], 0
    for ref, (teacher, first, count) in zip(piece_refs, pieces):
        done = 0
        while done < count:
            chunk = max(c for c in range(len(depths)) if starts[c] <= at)
            n = min(count - done, starts[chunk] + depths[chunk] - at)
            spans[chunk].append((ref, teacher, first + done, at - starts[chunk], n))
            at += n
            done += n
    empty = sum(depths) - at

    for c, depth in enumerate(depths):
        low = 2 * starts[c]
        for ref, teacher, first, at, n in spans[c]:
            units = ref.shape[0] // 3
            for k in range(2):
                gate_up[low + k * depth + at : low + k * depth + at + n, :] = ref[k * units + first : k * units + first + n, :]
            part = ref[2 * units + first : 2 * units + first + n, :]
            down[starts[c] + at : starts[c] + at + n, :] = -part if teacher else part
        if empty and c == len(depths) - 1:
            zeros = jnp.zeros((empty, width), BF16)
            for end in (low + depth, low + 2 * depth):
                gate_up[end - empty : end, :] = zeros
            down[starts[c] + depth - empty : starts[c] + depth, :] = zeros

        @pl.loop(0, rows // tile)
        def _(r, c=c, depth=depth, low=low):
            at = pl.ds(pl.multiple_of(r * tile, tile), tile)
            rows_in = x[at, :]
            turned = (((1,), (1,)), ((), ()))
            gate = lax.dot_general(rows_in, gate_up[low : low + depth], turned, preferred_element_type=F32)
            up = lax.dot_general(rows_in, gate_up[low + depth : low + 2 * depth], turned, preferred_element_type=F32)
            hidden = (gate / (1.0 + jnp.exp(-gate)) * up).astype(BF16)
            term = jnp.dot(hidden, down[starts[c] : starts[c] + depth], preferred_element_type=F32)
            within = pl.ds(pl.multiple_of(sum_at + r * tile, tile), tile)
            if not outs and (add or c > 0):
                sum_ref[within, :] += term
            elif not outs:
                sum_ref[within, :] = term
            else:
                term += acc_ref[within, :]
                ends = [sum(n for n, _ in outs[: i + 1]) for i in range(len(outs))]
                for t in range(rows // tile):

                    @pl.when(r == t)
                    def _(t=t):
                        for (n, dtype), end, ref in zip(outs, ends, out_refs):
                            if t * tile < end <= (t + 1) * tile:
                                ref[...] = term[end - n - t * tile : end - t * tile].astype(dtype)


def last_kernel(teacher, sum_at, halved, *refs):
    if halved:
        here_ref, *refs, held = refs
        refs, out_refs = refs[:-4], refs[-4:]
        *refs, sum_ref = refs
    else:
        *refs, sum_ref, out_ref = refs
    x_refs, piece_refs = refs[: -len(teacher)], refs[-len(teacher) :]
    x = x_refs[0][...] if len(x_refs) == 1 else jnp.concatenate([r[...] for r in x_refs], axis=0)
    total = sum_ref[sum_at : sum_at + x.shape[0], :]
    for ref, negative in zip(piece_refs, teacher):
        units = ref.shape[0] // 3
        wide = lax.dot_general(x, ref[: 2 * units], (((1,), (1,)), ((), ())), preferred_element_type=F32)
        gate, up = wide[:, :units], wide[:, units:]
        hidden = (gate / (1.0 + jnp.exp(-gate)) * up).astype(BF16)
        term = jnp.dot(hidden, ref[2 * units :], preferred_element_type=F32)
        total = total - term if negative else total + term
    if not halved:
        out_ref[...] = total.astype(out_ref.dtype)
        return
    held[...] = total
    for i, out_ref in enumerate(out_refs):
        for z in range(EXPERTS // 2):
            place = EXPERTS * (i // 2) + 2 * z + ((here_ref[0] + i) & 1)
            out_ref[z * CAP : (z + 1) * CAP] = held[block_of(place), :].astype(out_ref.dtype)


def last_net(xs, pieces, total, total_at, dtype, here=None):
    rows, width = sum(a.shape[0] for a in xs), xs[0].shape[1]
    halved = here is not None
    hidden = sum(p.shape[0] // 3 for p, _ in pieces)
    operands = list(xs) + [p for p, _ in pieces] + [total]
    return pl.pallas_call(
        functools.partial(last_kernel, tuple(t for _, t in pieces), total_at, halved),
        out_shape=[pltpu.VMEM((rows // 4, width), dtype)] * 4 if halved else pltpu.VMEM((rows, width), dtype),
        in_specs=(whole(1, pltpu.SMEM) if halved else []) + whole(len(operands)),
        out_specs=whole(4) if halved else whole(1)[0],
        scratch_shapes=[pltpu.VMEM((rows, width), F32)] if halved else [],
        compiler_params=params(),
        cost_estimate=pl.CostEstimate(
            flops=rows * width * hidden * 6, bytes_accessed=rows * width * 8 + hidden * width * 6, transcendentals=rows * hidden
        ),
        name="networks_last",
    )(*([here] if halved else []), *(near(a) for a in operands))


def net(xs, pieces, depths, tile, limit, total, total_at, add, outs=()):
    rows, width = sum(a.shape[0] for a in xs), xs[0].shape[1]
    fresh = isinstance(total, int)
    hidden = sum(depths)
    assert not outs or len(depths) == 1
    operands = list(xs) + [p[0] for p in pieces] + ([] if fresh else [total])
    shapes = outs or [(total if fresh else total.shape[0], F32)]
    return pl.pallas_call(
        functools.partial(net_kernel, len(xs), tuple(p[1:] for p in pieces), tuple(depths), total_at, add, tuple(outs), tile),
        out_shape=[pltpu.VMEM((n, width), d) for n, d in shapes],
        in_specs=whole(len(operands)),
        out_specs=whole(len(shapes)),
        input_output_aliases={} if fresh or outs else {len(operands) - 1: 0},
        scratch_shapes=[
            pltpu.VMEM((rows, width), BF16),
            pltpu.VMEM((2 * hidden, width), BF16),
            pltpu.VMEM((hidden, width), BF16),
        ],
        compiler_params=params(limit),
        cost_estimate=pl.CostEstimate(
            flops=rows * width * hidden * 6, bytes_accessed=rows * width * 8 + hidden * width * 6, transcendentals=rows * hidden
        ),
        name="networks",
    )(*(near(a) for a in operands))


def per_device(tokens, routes, gate_num, student_gate, student_up, student_down, teacher_gate, teacher_up, teacher_down):
    here = lax.axis_index("expert").astype(jnp.int32).reshape(1)
    routes, gate_num = routes.T, gate_num.T
    width = tokens.shape[1]
    units = student_gate.shape[2]
    block = EXPERTS * CAP
    half = block // 2
    mib = 1024 * 1024
    cut = units - 128

    student, rows = pack((student_gate[0], student_up[0], student_down[0]), routes, tokens)
    (teacher,) = pack((teacher_gate[0], teacher_up[0], teacher_down[0]))
    prev_student = send(student, ring(1, True))
    next_teacher = send(teacher, ring(-1, True))
    rows, teacher = barrier(rows, teacher)
    rows = rows.reshape(EXPERTS, CAP, width)
    rows = lax.all_to_all(rows, "expert", split_axis=0, concat_axis=0, tiled=True).reshape(block, width)

    prev_rows = send(rows, ring(1, False))
    next_rows = send(rows, ring(-1, False))
    first = [(student, False, 0, units), (teacher, True, 0, units), (prev_student, False, 0, units), (next_teacher, True, 0, units)]
    (total,) = net([rows], first, [512, 768], block, 28 * mib, 4 * block, 3 * block, False)

    parts = split(cut, barrier(student, total)[0], teacher)
    total, prev_student, next_teacher = barrier(total, prev_student, next_teacher)
    far_student = send(prev_student, ring(1, True))
    far_teacher = send(next_teacher, ring(-1, True))
    total, prev_rows, next_rows, *parts = barrier(total, prev_rows, next_rows, *parts)
    far_a = send(prev_rows[:half], ring(1, False))
    far_b = send(next_rows[half:], ring(-1, False))
    first = [(student, False, 0, units), (teacher, True, 0, units), (prev_student, False, 0, units), (next_teacher, True, 0, units)]
    near_xs = [next_rows, prev_rows]
    (total,) = net(near_xs, first, [512, 768], 2 * block, 32 * mib, total, block, False)

    total, far_a, far_b, *parts = barrier(total, far_a, far_b, *parts)
    student_a, student_b, teacher_a, teacher_b = parts
    prev_teacher_a = send(teacher_a, ring(1, True))
    next_student_a = send(student_a, ring(-1, True))
    far_xs = [far_a, far_b]
    (total,) = net(far_xs, first, [512, 768], block, 28 * mib, total, 0, False)
    high, low = shares(routes, gate_num)

    total, far_student, far_teacher, student_b, teacher_b = barrier(total, far_student, far_teacher, student_b, teacher_b)
    room = 512 - units
    second = [(far_student, False, 0, units), (far_teacher, True, 0, room)]
    third = [(far_teacher, True, room, units - room), (prev_teacher_a, True, 0, cut), (next_student_a, False, 0, cut)]
    last = [(send(teacher_b, ring(1, True)), True), (send(student_b, ring(-1, True)), False)]
    (total,) = net(far_xs + near_xs + [rows], second, [512], 2 * block, 24 * mib, total, 0, True)
    (total,) = net(far_xs + near_xs + [rows], third, [512], 2 * block, 24 * mib, total, 0, True)
    far_sum = last_net(far_xs, last, total, 0, BF16)
    total, far_sum = barrier(total, far_sum)
    far_sum = send(far_sum, ring(2, False))
    next_same, next_other, prev_same, prev_other = last_net(near_xs, last, total, block, BF16, here)
    total, _ = barrier(total, next_same)
    prev_part, prev_cross = send(next_same, ring(1, False)), send(next_other, cross(1))
    next_part, next_cross = send(prev_same, ring(-1, False)), send(prev_other, cross(-1))
    own = last_net([rows], last, total, 3 * block, F32)
    keep, give = halves(here, own, far_sum)
    given = send(give, cross(0))
    blocks = sum_rows(here, keep, prev_part, next_part, given, prev_cross, next_cross)
    return combine(here, high, low, [blocks[0]] + [send(blocks[step], along_z(step)) for step in range(1, EXPERTS // 2)])


def solution(mesh):
    in_specs = (
        P(("expert", "shard"), None),
        P(("expert", "shard"), None),
        P(("expert", "shard"), None),
        P("expert", None, "shard"),
        P("expert", None, "shard"),
        P("expert", "shard", None),
        P("expert", None, "shard"),
        P("expert", None, "shard"),
        P("expert", "shard", None),
    )
    out_specs = P(("expert", "shard"), None)
    return jax.shard_map(
        per_device, mesh=mesh, in_specs=in_specs, out_specs=out_specs, check_vma=False
    )
```

```python
import functools

import jax
import jax.numpy as jnp
from jax import lax
from jax.experimental import pallas as pl
from jax.experimental.pallas import tpu as pltpu
from jax.sharding import PartitionSpec as P

AXES = ("expert", "shard")
BF16 = jnp.bfloat16
F32 = jnp.float32
CAP = 48
EXPERTS = 8
VMEM_LIMIT = 16 * 1024 * 1024


def dev(z, c, y, x):
    return ((z % 4 * 2 + c % 2) * 4 + y % 4) * 4 + x % 4


COORDS = [(z, c, y, x) for z in range(4) for c in range(2) for y in range(4) for x in range(4)]


def ring(step, weights):
    return [
        (dev(z, c, y, x), dev(z, c, y, x + step) if (c == 0) == weights else dev(z, c, y + step, x))
        for z, c, y, x in COORDS
    ]


def cross(step):
    return [(dev(z, c, y, x), dev(z, 1 - c, y + step, x) if c == 0 else dev(z, 1 - c, y, x + step)) for z, c, y, x in COORDS]


def along_z(step):
    return [(dev(z, c, y, x), dev(z + step, c, y, x)) for z, c, y, x in COORDS]


def send(value, pairs):
    return lax.ppermute(value, AXES, pairs)


def barrier(*values):
    return lax.optimization_barrier(values)


def whole(count, space=pltpu.VMEM):
    return [pl.BlockSpec(memory_space=space)] * count


def params(limit=VMEM_LIMIT):
    return pltpu.CompilerParams(vmem_limit_bytes=limit)


def near(value):
    return pltpu.with_memory_space_constraint(value, pltpu.VMEM)


def places(routes_ref):
    tokens = routes_ref.shape[1]
    first, second = routes_ref[0:1, :], routes_ref[1:2, :]
    expert = lax.broadcasted_iota(jnp.int32, (16, tokens), 0)
    named = ((expert == first).astype(F32) + (expert == second).astype(F32)).astype(BF16)
    before = lax.broadcasted_iota(jnp.int32, (tokens, tokens), 0) < lax.broadcasted_iota(jnp.int32, (tokens, tokens), 1)
    earlier = jnp.dot(named, before.astype(F32).astype(BF16), preferred_element_type=F32)
    found = []
    for ids, extra in ((first, 0), (second, (first == second).astype(jnp.int32))):
        slot = jnp.sum(jnp.where(expert == ids, earlier, 0.0), axis=0, keepdims=True).astype(jnp.int32) + extra
        found.append(ids * CAP + slot)
    return found


def pack_kernel(n_rest, *refs):
    weight_refs, rest, packed_ref = refs[:3], refs[3 : 3 + n_rest], refs[3 + n_rest]
    sems = refs[-1]
    units = weight_refs[0].shape[0]
    ins = [
        pltpu.make_async_copy(ref, packed_ref.at[pl.ds(i * units, units)], sems.at[i]) for i, ref in enumerate(weight_refs)
    ]
    for copy in ins:
        copy.start()
    if rest:
        routes_ref, tokens_ref = rest
        first, second = places(routes_ref)
        slots = lax.broadcasted_iota(jnp.int32, (EXPERTS * CAP, tokens_ref.shape[0]), 0)
        chosen = ((slots == first) | (slots == second)).astype(F32).astype(BF16)
        refs[4 + n_rest][...] = jnp.dot(chosen, tokens_ref[...], preferred_element_type=F32).astype(BF16)
    for copy in ins:
        copy.wait()


def pack(weights, *rest):
    gate, up, down = weights
    units, width = down.shape
    rows = [pltpu.VMEM((EXPERTS * CAP, width), BF16)] if rest else []
    return pl.pallas_call(
        functools.partial(pack_kernel, len(rest)),
        out_shape=[pltpu.VMEM((3 * units, width), BF16)] + rows,
        in_specs=whole(3, pltpu.HBM) + whole(len(rest)),
        out_specs=whole(1 + len(rows)),
        scratch_shapes=[pltpu.SemaphoreType.DMA((3,))],
        compiler_params=params(58 * 1024 * 1024 if rest else VMEM_LIMIT),
        cost_estimate=pl.CostEstimate(flops=100_000_000, bytes_accessed=4_000_000, transcendentals=0),
        name="pack_weights",
    )(gate.T, up.T, down, *rest)


def split_kernel(cut, *refs):
    n = len(refs) // 3
    for i in range(n):
        units = refs[i].shape[0] // 3
        for ref, first, count in ((refs[n + 2 * i], 0, cut), (refs[n + 2 * i + 1], cut, units - cut)):
            for k in range(3):
                ref[k * count : (k + 1) * count] = refs[i][k * units + first : k * units + first + count]


def split(cut, *packed):
    shapes = [pltpu.VMEM((3 * n, p.shape[1]), BF16) for p in packed for n in (cut, p.shape[0] // 3 - cut)]
    return pl.pallas_call(
        functools.partial(split_kernel, cut),
        out_shape=shapes,
        in_specs=whole(len(packed)),
        out_specs=whole(len(shapes)),
        compiler_params=params(),
        cost_estimate=pl.CostEstimate(flops=0, bytes_accessed=6_000_000, transcendentals=0),
        name="split_weights",
    )(*(near(p) for p in packed))


def shares_kernel(routes_ref, gates_ref, high_ref, low_ref):
    first, second = places(routes_ref)
    gates = gates_ref[...].astype(F32)
    share = gates / jnp.sum(gates, axis=0, keepdims=True)
    slots = lax.broadcasted_iota(jnp.int32, (EXPERTS * CAP, routes_ref.shape[1]), 0)
    weight = jnp.where(slots == first, share[0:1], 0.0) + jnp.where(slots == second, share[1:2], 0.0)
    weight = weight.T
    high = weight.astype(BF16)
    high_ref[...] = high
    low_ref[...] = (weight - high.astype(F32)).astype(BF16)


def shares(routes, gates):
    tokens = routes.shape[1]
    return pl.pallas_call(
        shares_kernel,
        out_shape=[jax.ShapeDtypeStruct((tokens, EXPERTS * CAP), BF16)] * 2,
        in_specs=whole(2),
        out_specs=whole(2),
        compiler_params=params(),
        cost_estimate=pl.CostEstimate(flops=10_000_000, bytes_accessed=1_000_000, transcendentals=0),
        name="gate_shares",
    )(routes, gates)


def block_of(place):
    return pl.ds(pl.multiple_of(place * CAP, CAP), CAP)


def halves_kernel(here_ref, own_ref, far_ref, keep_ref, give_ref):
    core = here_ref[0] & 1
    for z in range(EXPERTS // 2):
        to = slice(z * CAP, (z + 1) * CAP)
        at = block_of(2 * z + core)
        keep_ref[to] = own_ref[at, :] + far_ref[at, :].astype(F32)
        at = block_of(2 * z + 1 - core)
        give_ref[to] = (own_ref[at, :] + far_ref[at, :].astype(F32)).astype(BF16)


def halves(here, own, far_part):
    rows, width = own.shape
    return pl.pallas_call(
        halves_kernel,
        out_shape=[pltpu.VMEM((rows // 2, width), F32), pltpu.VMEM((rows // 2, width), BF16)],
        in_specs=whole(1, pltpu.SMEM) + whole(2),
        out_specs=whole(2),
        compiler_params=params(),
        cost_estimate=pl.CostEstimate(flops=1_000_000, bytes_accessed=3_000_000, transcendentals=0),
        name="halve_rows",
    )(here, near(own), near(far_part))


def sum_kernel(here_ref, keep_ref, prev_ref, next_ref, given_ref, prev_other_ref, next_other_ref, *out_refs):
    z = here_ref[0] >> 1
    for step, out_ref in enumerate(out_refs):
        at = block_of((z + step) & 3)
        mine = keep_ref[at, :] + prev_ref[at, :].astype(F32) + next_ref[at, :].astype(F32)
        other = given_ref[at, :].astype(F32) + prev_other_ref[at, :].astype(F32) + next_other_ref[at, :].astype(F32)
        out_ref[:CAP] = mine.astype(BF16)
        out_ref[CAP:] = other.astype(BF16)


def sum_rows(here, *parts):
    steps, width = EXPERTS // 2, parts[0].shape[1]
    return pl.pallas_call(
        sum_kernel,
        out_shape=[pltpu.VMEM((2 * CAP, width), BF16)] * steps,
        in_specs=whole(1, pltpu.SMEM) + whole(len(parts)),
        out_specs=whole(steps),
        compiler_params=params(),
        cost_estimate=pl.CostEstimate(flops=1_000_000, bytes_accessed=4_000_000, transcendentals=0),
        name="sum_rows",
    )(here, *(near(p) for p in parts))


def combine_kernel(here_ref, high_ref, low_ref, *refs):
    *block_refs, out_ref, held = refs
    z, core = here_ref[0] >> 1, here_ref[0] & 1
    for step, ref in enumerate(block_refs):
        chip = 2 * ((z - step) & 3)
        held[block_of(chip + core), :] = ref[:CAP]
        held[block_of(chip + 1 - core), :] = ref[CAP:]
    rows = held[...]
    total = jnp.dot(high_ref[...], rows, preferred_element_type=F32)
    total += jnp.dot(low_ref[...], rows, preferred_element_type=F32)
    out_ref[...] = total.astype(BF16)


def combine(here, high, low, blocks):
    tokens, width = high.shape[0], blocks[0].shape[1]
    return pl.pallas_call(
        combine_kernel,
        out_shape=jax.ShapeDtypeStruct((tokens, width), BF16),
        in_specs=whole(1, pltpu.SMEM) + whole(2 + len(blocks)),
        out_specs=pl.BlockSpec(memory_space=pltpu.VMEM),
        scratch_shapes=[pltpu.VMEM((EXPERTS * CAP, width), BF16)],
        compiler_params=params(),
        cost_estimate=pl.CostEstimate(flops=200_000_000, bytes_accessed=1_000_000, transcendentals=0),
        name="combine_rows",
    )(here, near(high), near(low), *(near(b) for b in blocks))


def net_kernel(n_x, pieces, depths, sum_at, add, outs, tile, *refs):
    x_refs, refs = refs[:n_x], refs[n_x:]
    piece_refs, refs = refs[: len(pieces)], refs[len(pieces) :]
    n_sums = len(refs) - max(len(outs), 1) - 3
    if n_sums:
        acc_ref, refs = refs[0], refs[1:]
    if outs:
        out_refs, refs = refs[: len(outs)], refs[len(outs) :]
    else:
        sum_ref, refs = refs[0], refs[1:]
    x, gate_up, down = refs
    rows, width = x.shape
    starts = [sum(depths[:c]) for c in range(len(depths))]

    at = 0
    for ref in x_refs:
        x[at : at + ref.shape[0], :] = ref[...]
        at += ref.shape[0]

    spans, at = [[] for _ in depths], 0
    for ref, (teacher, first, count) in zip(piece_refs, pieces):
        done = 0
        while done < count:
            chunk = max(c for c in range(len(depths)) if starts[c] <= at)
            n = min(count - done, starts[chunk] + depths[chunk] - at)
            spans[chunk].append((ref, teacher, first + done, at - starts[chunk], n))
            at += n
            done += n
    empty = sum(depths) - at

    for c, depth in enumerate(depths):
        low = 2 * starts[c]
        for ref, teacher, first, at, n in spans[c]:
            units = ref.shape[0] // 3
            for k in range(2):
                gate_up[low + k * depth + at : low + k * depth + at + n, :] = ref[k * units + first : k * units + first + n, :]
            part = ref[2 * units + first : 2 * units + first + n, :]
            down[starts[c] + at : starts[c] + at + n, :] = -part if teacher else part
        if empty and c == len(depths) - 1:
            zeros = jnp.zeros((empty, width), BF16)
            for end in (low + depth, low + 2 * depth):
                gate_up[end - empty : end, :] = zeros
            down[starts[c] + depth - empty : starts[c] + depth, :] = zeros

        @pl.loop(0, rows // tile)
        def _(r, c=c, depth=depth, low=low):
            at = pl.ds(pl.multiple_of(r * tile, tile), tile)
            rows_in = x[at, :]
            turned = (((1,), (1,)), ((), ()))
            gate = lax.dot_general(rows_in, gate_up[low : low + depth], turned, preferred_element_type=F32)
            up = lax.dot_general(rows_in, gate_up[low + depth : low + 2 * depth], turned, preferred_element_type=F32)
            hidden = (gate / (1.0 + jnp.exp(-gate)) * up).astype(BF16)
            term = jnp.dot(hidden, down[starts[c] : starts[c] + depth], preferred_element_type=F32)
            within = pl.ds(pl.multiple_of(sum_at + r * tile, tile), tile)
            if not outs and (add or c > 0):
                sum_ref[within, :] += term
            elif not outs:
                sum_ref[within, :] = term
            else:
                term += acc_ref[within, :]
                ends = [sum(n for n, _ in outs[: i + 1]) for i in range(len(outs))]
                for t in range(rows // tile):

                    @pl.when(r == t)
                    def _(t=t):
                        for (n, dtype), end, ref in zip(outs, ends, out_refs):
                            if t * tile < end <= (t + 1) * tile:
                                ref[...] = term[end - n - t * tile : end - t * tile].astype(dtype)


def last_kernel(teacher, sum_at, halved, *refs):
    if halved:
        here_ref, *refs, held = refs
        refs, out_refs = refs[:-4], refs[-4:]
        *refs, sum_ref = refs
    else:
        *refs, sum_ref, out_ref = refs
    x_refs, piece_refs = refs[: -len(teacher)], refs[-len(teacher) :]
    x = x_refs[0][...] if len(x_refs) == 1 else jnp.concatenate([r[...] for r in x_refs], axis=0)
    units = piece_refs[0].shape[0] // 3
    turned = (((1,), (1,)), ((), ()))
    gate = lax.dot_general(x, jnp.concatenate([r[:units] for r in piece_refs], axis=0), turned, preferred_element_type=F32)
    up = lax.dot_general(x, jnp.concatenate([r[units : 2 * units] for r in piece_refs], axis=0), turned, preferred_element_type=F32)
    hidden = (gate / (1.0 + jnp.exp(-gate)) * up).astype(BF16)
    down = jnp.concatenate([-r[2 * units :] if negative else r[2 * units :] for r, negative in zip(piece_refs, teacher)], axis=0)
    total = sum_ref[sum_at : sum_at + x.shape[0], :] + jnp.dot(hidden, down, preferred_element_type=F32)
    if not halved:
        out_ref[...] = total.astype(out_ref.dtype)
        return
    held[...] = total
    for i, out_ref in enumerate(out_refs):
        for z in range(EXPERTS // 2):
            place = EXPERTS * (i // 2) + 2 * z + ((here_ref[0] + i) & 1)
            out_ref[z * CAP : (z + 1) * CAP] = held[block_of(place), :].astype(out_ref.dtype)


def last_net(xs, pieces, total, total_at, dtype, here=None):
    rows, width = sum(a.shape[0] for a in xs), xs[0].shape[1]
    halved = here is not None
    hidden = sum(p.shape[0] // 3 for p, _ in pieces)
    operands = list(xs) + [p for p, _ in pieces] + [total]
    return pl.pallas_call(
        functools.partial(last_kernel, tuple(t for _, t in pieces), total_at, halved),
        out_shape=[pltpu.VMEM((rows // 4, width), dtype)] * 4 if halved else pltpu.VMEM((rows, width), dtype),
        in_specs=(whole(1, pltpu.SMEM) if halved else []) + whole(len(operands)),
        out_specs=whole(4) if halved else whole(1)[0],
        scratch_shapes=[pltpu.VMEM((rows, width), F32)] if halved else [],
        compiler_params=params(),
        cost_estimate=pl.CostEstimate(
            flops=rows * width * hidden * 6, bytes_accessed=rows * width * 8 + hidden * width * 6, transcendentals=rows * hidden
        ),
        name="networks_last",
    )(*([here] if halved else []), *(near(a) for a in operands))


def net(xs, pieces, depths, tile, limit, total, total_at, add, outs=()):
    rows, width = sum(a.shape[0] for a in xs), xs[0].shape[1]
    fresh = isinstance(total, int)
    hidden = sum(depths)
    assert not outs or len(depths) == 1
    operands = list(xs) + [p[0] for p in pieces] + ([] if fresh else [total])
    shapes = outs or [(total if fresh else total.shape[0], F32)]
    return pl.pallas_call(
        functools.partial(net_kernel, len(xs), tuple(p[1:] for p in pieces), tuple(depths), total_at, add, tuple(outs), tile),
        out_shape=[pltpu.VMEM((n, width), d) for n, d in shapes],
        in_specs=whole(len(operands)),
        out_specs=whole(len(shapes)),
        input_output_aliases={} if fresh or outs else {len(operands) - 1: 0},
        scratch_shapes=[
            pltpu.VMEM((rows, width), BF16),
            pltpu.VMEM((2 * hidden, width), BF16),
            pltpu.VMEM((hidden, width), BF16),
        ],
        compiler_params=params(limit),
        cost_estimate=pl.CostEstimate(
            flops=rows * width * hidden * 6, bytes_accessed=rows * width * 8 + hidden * width * 6, transcendentals=rows * hidden
        ),
        name="networks",
    )(*(near(a) for a in operands))


def per_device(tokens, routes, gate_num, student_gate, student_up, student_down, teacher_gate, teacher_up, teacher_down):
    here = lax.axis_index("expert").astype(jnp.int32).reshape(1)
    routes, gate_num = routes.T, gate_num.T
    width = tokens.shape[1]
    units = student_gate.shape[2]
    block = EXPERTS * CAP
    half = block // 2
    mib = 1024 * 1024
    cut = units - 128

    student, rows = pack((student_gate[0], student_up[0], student_down[0]), routes, tokens)
    (teacher,) = pack((teacher_gate[0], teacher_up[0], teacher_down[0]))
    prev_student = send(student, ring(1, True))
    next_teacher = send(teacher, ring(-1, True))
    rows, teacher = barrier(rows, teacher)
    rows = rows.reshape(EXPERTS, CAP, width)
    rows = lax.all_to_all(rows, "expert", split_axis=0, concat_axis=0, tiled=True).reshape(block, width)

    prev_rows = send(rows, ring(1, False))
    next_rows = send(rows, ring(-1, False))
    first = [(student, False, 0, units), (teacher, True, 0, units), (prev_student, False, 0, units), (next_teacher, True, 0, units)]
    (total,) = net([rows], first, [512, 768], block, 28 * mib, 4 * block, 3 * block, False)

    parts = split(cut, barrier(student, total)[0], teacher)
    total, prev_student, next_teacher = barrier(total, prev_student, next_teacher)
    far_student = send(prev_student, ring(1, True))
    far_teacher = send(next_teacher, ring(-1, True))
    total, prev_rows, next_rows, *parts = barrier(total, prev_rows, next_rows, *parts)
    far_a = send(prev_rows[:half], ring(1, False))
    far_b = send(next_rows[half:], ring(-1, False))
    first = [(student, False, 0, units), (teacher, True, 0, units), (prev_student, False, 0, units), (next_teacher, True, 0, units)]
    near_xs = [next_rows, prev_rows]
    (total,) = net(near_xs, first, [512, 768], 2 * block, 32 * mib, total, block, False)

    total, *parts = barrier(total, *parts)
    student_a, student_b, teacher_a, teacher_b = parts
    prev_teacher_a = send(teacher_a, ring(1, True))
    next_student_a = send(student_a, ring(-1, True))
    far_xs = [far_a, far_b]
    (total,) = net(far_xs, first, [512, 768], block, 28 * mib, total, 0, False)
    high, low = shares(routes, gate_num)

    total, far_student, far_teacher, student_b, teacher_b = barrier(total, far_student, far_teacher, student_b, teacher_b)
    room = 512 - units
    second = [(far_student, False, 0, units), (far_teacher, True, 0, room)]
    third = [(far_teacher, True, room, units - room), (prev_teacher_a, True, 0, cut), (next_student_a, False, 0, cut)]
    last = [(send(teacher_b, ring(1, True)), True), (send(student_b, ring(-1, True)), False)]
    (total,) = net(far_xs + near_xs + [rows], second, [512], 2 * block, 24 * mib, total, 0, True)
    (total,) = net(far_xs + near_xs + [rows], third, [512], 2 * block, 24 * mib, total, 0, True)
    far_sum = last_net(far_xs, last, total, 0, BF16)
    total, far_sum = barrier(total, far_sum)
    far_sum = send(far_sum, ring(2, False))
    next_same, next_other, prev_same, prev_other = last_net(near_xs, last, total, block, BF16, here)
    total, _ = barrier(total, next_same)
    prev_part, prev_cross = send(next_same, ring(1, False)), send(next_other, cross(1))
    next_part, next_cross = send(prev_same, ring(-1, False)), send(prev_other, cross(-1))
    own = last_net([rows], last, total, 3 * block, F32)
    keep, give = halves(here, own, far_sum)
    given = send(give, cross(0))
    blocks = sum_rows(here, keep, prev_part, next_part, given, prev_cross, next_cross)
    across = send(blocks[2], along_z(2))
    return combine(here, high, low, [blocks[0], send(blocks[1], along_z(1)), across, send(blocks[3], along_z(3))])


def solution(mesh):
    in_specs = (
        P(("expert", "shard"), None),
        P(("expert", "shard"), None),
        P(("expert", "shard"), None),
        P("expert", None, "shard"),
        P("expert", None, "shard"),
        P("expert", "shard", None),
        P("expert", None, "shard"),
        P("expert", None, "shard"),
        P("expert", "shard", None),
    )
    out_specs = P(("expert", "shard"), None)
    return jax.shard_map(
        per_device, mesh=mesh, in_specs=in_specs, out_specs=out_specs, check_vma=False
    )
```

```python
import functools

import jax
import jax.numpy as jnp
from jax import lax
from jax.experimental import pallas as pl
from jax.experimental.pallas import tpu as pltpu
from jax.sharding import PartitionSpec as P

AXES = ("expert", "shard")
BF16 = jnp.bfloat16
F32 = jnp.float32
CAP = 48
EXPERTS = 8
STEPS = (2, 1, 3, 0)
VMEM_LIMIT = 16 * 1024 * 1024


def dev(z, c, y, x):
    return ((z % 4 * 2 + c % 2) * 4 + y % 4) * 4 + x % 4


COORDS = [(z, c, y, x) for z in range(4) for c in range(2) for y in range(4) for x in range(4)]


def ring(step, weights):
    return [
        (dev(z, c, y, x), dev(z, c, y, x + step) if (c == 0) == weights else dev(z, c, y + step, x))
        for z, c, y, x in COORDS
    ]


def cross(step):
    return [(dev(z, c, y, x), dev(z, 1 - c, y + step, x) if c == 0 else dev(z, 1 - c, y, x + step)) for z, c, y, x in COORDS]


def along_z(step):
    return [(dev(z, c, y, x), dev(z + step, c, y, x)) for z, c, y, x in COORDS]


def send(value, pairs):
    return lax.ppermute(value, AXES, pairs)


def barrier(*values):
    return lax.optimization_barrier(values)


def whole(count, space=pltpu.VMEM):
    return [pl.BlockSpec(memory_space=space)] * count


def params(limit=VMEM_LIMIT):
    return pltpu.CompilerParams(vmem_limit_bytes=limit)


def near(value):
    return pltpu.with_memory_space_constraint(value, pltpu.VMEM)


def places(routes_ref):
    tokens = routes_ref.shape[1]
    first, second = routes_ref[0:1, :], routes_ref[1:2, :]
    expert = lax.broadcasted_iota(jnp.int32, (16, tokens), 0)
    named = ((expert == first).astype(F32) + (expert == second).astype(F32)).astype(BF16)
    before = lax.broadcasted_iota(jnp.int32, (tokens, tokens), 0) < lax.broadcasted_iota(jnp.int32, (tokens, tokens), 1)
    earlier = jnp.dot(named, before.astype(F32).astype(BF16), preferred_element_type=F32)
    found = []
    for ids, extra in ((first, 0), (second, (first == second).astype(jnp.int32))):
        slot = jnp.sum(jnp.where(expert == ids, earlier, 0.0), axis=0, keepdims=True).astype(jnp.int32) + extra
        found.append(ids * CAP + slot)
    return found


def pack_kernel(n_rest, *refs):
    weight_refs, rest, packed_ref = refs[:3], refs[3 : 3 + n_rest], refs[3 + n_rest]
    sems = refs[-1]
    units = weight_refs[0].shape[0]
    ins = [
        pltpu.make_async_copy(ref, packed_ref.at[pl.ds(i * units, units)], sems.at[i]) for i, ref in enumerate(weight_refs)
    ]
    for copy in ins:
        copy.start()
    if rest:
        routes_ref, tokens_ref = rest
        first, second = places(routes_ref)
        slots = lax.broadcasted_iota(jnp.int32, (EXPERTS * CAP, tokens_ref.shape[0]), 0)
        chosen = ((slots == first) | (slots == second)).astype(F32).astype(BF16)
        refs[4 + n_rest][...] = jnp.dot(chosen, tokens_ref[...], preferred_element_type=F32).astype(BF16)
    for copy in ins:
        copy.wait()


def pack(weights, *rest):
    gate, up, down = weights
    units, width = down.shape
    rows = [pltpu.VMEM((EXPERTS * CAP, width), BF16)] if rest else []
    return pl.pallas_call(
        functools.partial(pack_kernel, len(rest)),
        out_shape=[pltpu.VMEM((3 * units, width), BF16)] + rows,
        in_specs=whole(3, pltpu.HBM) + whole(len(rest)),
        out_specs=whole(1 + len(rows)),
        scratch_shapes=[pltpu.SemaphoreType.DMA((3,))],
        compiler_params=params(58 * 1024 * 1024 if rest else VMEM_LIMIT),
        cost_estimate=pl.CostEstimate(flops=100_000_000, bytes_accessed=4_000_000, transcendentals=0),
        name="pack_weights",
    )(gate.T, up.T, down, *rest)


def split_kernel(cut, *refs):
    n = len(refs) // 3
    for i in range(n):
        units = refs[i].shape[0] // 3
        for ref, first, count in ((refs[n + 2 * i], 0, cut), (refs[n + 2 * i + 1], cut, units - cut)):
            for k in range(3):
                ref[k * count : (k + 1) * count] = refs[i][k * units + first : k * units + first + count]


def split(cut, *packed):
    shapes = [pltpu.VMEM((3 * n, p.shape[1]), BF16) for p in packed for n in (cut, p.shape[0] // 3 - cut)]
    return pl.pallas_call(
        functools.partial(split_kernel, cut),
        out_shape=shapes,
        in_specs=whole(len(packed)),
        out_specs=whole(len(shapes)),
        compiler_params=params(),
        cost_estimate=pl.CostEstimate(flops=0, bytes_accessed=6_000_000, transcendentals=0),
        name="split_weights",
    )(*(near(p) for p in packed))


def shares_kernel(routes_ref, gates_ref, high_ref, low_ref):
    first, second = places(routes_ref)
    gates = gates_ref[...].astype(F32)
    share = gates / jnp.sum(gates, axis=0, keepdims=True)
    slots = lax.broadcasted_iota(jnp.int32, (EXPERTS * CAP, routes_ref.shape[1]), 0)
    weight = jnp.where(slots == first, share[0:1], 0.0) + jnp.where(slots == second, share[1:2], 0.0)
    weight = weight.T
    high = weight.astype(BF16)
    high_ref[...] = high
    low_ref[...] = (weight - high.astype(F32)).astype(BF16)


def shares(routes, gates):
    tokens = routes.shape[1]
    return pl.pallas_call(
        shares_kernel,
        out_shape=[jax.ShapeDtypeStruct((tokens, EXPERTS * CAP), BF16)] * 2,
        in_specs=whole(2),
        out_specs=whole(2),
        compiler_params=params(),
        cost_estimate=pl.CostEstimate(flops=10_000_000, bytes_accessed=1_000_000, transcendentals=0),
        name="gate_shares",
    )(routes, gates)


def block_of(place):
    return pl.ds(pl.multiple_of(place * CAP, CAP), CAP)


def halves_kernel(here_ref, own_ref, far_ref, keep_ref, give_ref):
    core = here_ref[0] & 1
    for z in range(EXPERTS // 2):
        to = slice(z * CAP, (z + 1) * CAP)
        at = block_of(2 * z + core)
        keep_ref[to] = own_ref[at, :] + far_ref[at, :].astype(F32)
        at = block_of(2 * z + 1 - core)
        give_ref[to] = (own_ref[at, :] + far_ref[at, :].astype(F32)).astype(BF16)


def halves(here, own, far_part):
    rows, width = own.shape
    return pl.pallas_call(
        halves_kernel,
        out_shape=[pltpu.VMEM((rows // 2, width), F32), pltpu.VMEM((rows // 2, width), BF16)],
        in_specs=whole(1, pltpu.SMEM) + whole(2),
        out_specs=whole(2),
        compiler_params=params(),
        cost_estimate=pl.CostEstimate(flops=1_000_000, bytes_accessed=3_000_000, transcendentals=0),
        name="halve_rows",
    )(here, near(own), near(far_part))


def sum_kernel(here_ref, keep_ref, prev_ref, next_ref, given_ref, prev_other_ref, next_other_ref, *out_refs):
    z = here_ref[0] >> 1
    for step, out_ref in enumerate(out_refs):
        at = block_of((z + step) & 3)
        mine = keep_ref[at, :] + prev_ref[at, :].astype(F32) + next_ref[at, :].astype(F32)
        other = given_ref[at, :].astype(F32) + prev_other_ref[at, :].astype(F32) + next_other_ref[at, :].astype(F32)
        out_ref[:CAP] = mine.astype(BF16)
        out_ref[CAP:] = other.astype(BF16)


def sum_rows(here, *parts):
    steps, width = EXPERTS // 2, parts[0].shape[1]
    return pl.pallas_call(
        sum_kernel,
        out_shape=[pltpu.VMEM((2 * CAP, width), BF16)] * steps,
        in_specs=whole(1, pltpu.SMEM) + whole(len(parts)),
        out_specs=whole(steps),
        compiler_params=params(),
        cost_estimate=pl.CostEstimate(flops=1_000_000, bytes_accessed=4_000_000, transcendentals=0),
        name="sum_rows",
    )(here, *(near(p) for p in parts))


def combine_kernel(here_ref, high_ref, low_ref, *refs):
    *block_refs, out_ref, held = refs
    z, core = here_ref[0] >> 1, here_ref[0] & 1
    for step, ref in zip(STEPS, block_refs):
        chip = 2 * ((z - step) & 3)
        held[block_of(chip + core), :] = ref[:CAP]
        held[block_of(chip + 1 - core), :] = ref[CAP:]
    rows = held[...]
    total = jnp.dot(high_ref[...], rows, preferred_element_type=F32)
    total += jnp.dot(low_ref[...], rows, preferred_element_type=F32)
    out_ref[...] = total.astype(BF16)


def combine(here, high, low, blocks):
    tokens, width = high.shape[0], blocks[0].shape[1]
    return pl.pallas_call(
        combine_kernel,
        out_shape=jax.ShapeDtypeStruct((tokens, width), BF16),
        in_specs=whole(1, pltpu.SMEM) + whole(2 + len(blocks)),
        out_specs=pl.BlockSpec(memory_space=pltpu.VMEM),
        scratch_shapes=[pltpu.VMEM((EXPERTS * CAP, width), BF16)],
        compiler_params=params(),
        cost_estimate=pl.CostEstimate(flops=200_000_000, bytes_accessed=1_000_000, transcendentals=0),
        name="combine_rows",
    )(here, near(high), near(low), *(near(b) for b in blocks))


def net_kernel(n_x, pieces, depths, sum_at, add, outs, tile, *refs):
    x_refs, refs = refs[:n_x], refs[n_x:]
    piece_refs, refs = refs[: len(pieces)], refs[len(pieces) :]
    n_sums = len(refs) - max(len(outs), 1) - 3
    if n_sums:
        acc_ref, refs = refs[0], refs[1:]
    if outs:
        out_refs, refs = refs[: len(outs)], refs[len(outs) :]
    else:
        sum_ref, refs = refs[0], refs[1:]
    x, gate_up, down = refs
    rows, width = x.shape
    starts = [sum(depths[:c]) for c in range(len(depths))]

    at = 0
    for ref in x_refs:
        x[at : at + ref.shape[0], :] = ref[...]
        at += ref.shape[0]

    spans, at = [[] for _ in depths], 0
    for ref, (teacher, first, count) in zip(piece_refs, pieces):
        done = 0
        while done < count:
            chunk = max(c for c in range(len(depths)) if starts[c] <= at)
            n = min(count - done, starts[chunk] + depths[chunk] - at)
            spans[chunk].append((ref, teacher, first + done, at - starts[chunk], n))
            at += n
            done += n
    empty = sum(depths) - at

    for c, depth in enumerate(depths):
        low = 2 * starts[c]
        for ref, teacher, first, at, n in spans[c]:
            units = ref.shape[0] // 3
            for k in range(2):
                gate_up[low + k * depth + at : low + k * depth + at + n, :] = ref[k * units + first : k * units + first + n, :]
            part = ref[2 * units + first : 2 * units + first + n, :]
            down[starts[c] + at : starts[c] + at + n, :] = -part if teacher else part
        if empty and c == len(depths) - 1:
            zeros = jnp.zeros((empty, width), BF16)
            for end in (low + depth, low + 2 * depth):
                gate_up[end - empty : end, :] = zeros
            down[starts[c] + depth - empty : starts[c] + depth, :] = zeros

        @pl.loop(0, rows // tile)
        def _(r, c=c, depth=depth, low=low):
            at = pl.ds(pl.multiple_of(r * tile, tile), tile)
            rows_in = x[at, :]
            turned = (((1,), (1,)), ((), ()))
            gate = lax.dot_general(rows_in, gate_up[low : low + depth], turned, preferred_element_type=F32)
            up = lax.dot_general(rows_in, gate_up[low + depth : low + 2 * depth], turned, preferred_element_type=F32)
            hidden = (gate / (1.0 + jnp.exp(-gate)) * up).astype(BF16)
            term = jnp.dot(hidden, down[starts[c] : starts[c] + depth], preferred_element_type=F32)
            within = pl.ds(pl.multiple_of(sum_at + r * tile, tile), tile)
            if not outs and (add or c > 0):
                sum_ref[within, :] += term
            elif not outs:
                sum_ref[within, :] = term
            else:
                term += acc_ref[within, :]
                ends = [sum(n for n, _ in outs[: i + 1]) for i in range(len(outs))]
                for t in range(rows // tile):

                    @pl.when(r == t)
                    def _(t=t):
                        for (n, dtype), end, ref in zip(outs, ends, out_refs):
                            if t * tile < end <= (t + 1) * tile:
                                ref[...] = term[end - n - t * tile : end - t * tile].astype(dtype)


def last_kernel(teacher, sum_at, halved, *refs):
    if halved:
        here_ref, *refs, held = refs
        refs, out_refs = refs[:-4], refs[-4:]
        *refs, sum_ref = refs
    else:
        *refs, sum_ref, out_ref = refs
    x_refs, piece_refs = refs[: -len(teacher)], refs[-len(teacher) :]
    x = x_refs[0][...] if len(x_refs) == 1 else jnp.concatenate([r[...] for r in x_refs], axis=0)
    units = piece_refs[0].shape[0] // 3
    turned = (((1,), (1,)), ((), ()))
    gate = lax.dot_general(x, jnp.concatenate([r[:units] for r in piece_refs], axis=0), turned, preferred_element_type=F32)
    up = lax.dot_general(x, jnp.concatenate([r[units : 2 * units] for r in piece_refs], axis=0), turned, preferred_element_type=F32)
    hidden = (gate / (1.0 + jnp.exp(-gate)) * up).astype(BF16)
    down = jnp.concatenate([-r[2 * units :] if negative else r[2 * units :] for r, negative in zip(piece_refs, teacher)], axis=0)
    total = sum_ref[sum_at : sum_at + x.shape[0], :] + jnp.dot(hidden, down, preferred_element_type=F32)
    if not halved:
        out_ref[...] = total.astype(out_ref.dtype)
        return
    held[...] = total
    for i, out_ref in enumerate(out_refs):
        for z in range(EXPERTS // 2):
            place = EXPERTS * (i // 2) + 2 * z + ((here_ref[0] + i) & 1)
            out_ref[z * CAP : (z + 1) * CAP] = held[block_of(place), :].astype(out_ref.dtype)


def last_net(xs, pieces, total, total_at, dtype, here=None):
    rows, width = sum(a.shape[0] for a in xs), xs[0].shape[1]
    halved = here is not None
    hidden = sum(p.shape[0] // 3 for p, _ in pieces)
    operands = list(xs) + [p for p, _ in pieces] + [total]
    return pl.pallas_call(
        functools.partial(last_kernel, tuple(t for _, t in pieces), total_at, halved),
        out_shape=[pltpu.VMEM((rows // 4, width), dtype)] * 4 if halved else pltpu.VMEM((rows, width), dtype),
        in_specs=(whole(1, pltpu.SMEM) if halved else []) + whole(len(operands)),
        out_specs=whole(4) if halved else whole(1)[0],
        scratch_shapes=[pltpu.VMEM((rows, width), F32)] if halved else [],
        compiler_params=params(),
        cost_estimate=pl.CostEstimate(
            flops=rows * width * hidden * 6, bytes_accessed=rows * width * 8 + hidden * width * 6, transcendentals=rows * hidden
        ),
        name="networks_last",
    )(*([here] if halved else []), *(near(a) for a in operands))


def net(xs, pieces, depths, tile, limit, total, total_at, add, outs=()):
    rows, width = sum(a.shape[0] for a in xs), xs[0].shape[1]
    fresh = isinstance(total, int)
    hidden = sum(depths)
    assert not outs or len(depths) == 1
    operands = list(xs) + [p[0] for p in pieces] + ([] if fresh else [total])
    shapes = outs or [(total if fresh else total.shape[0], F32)]
    return pl.pallas_call(
        functools.partial(net_kernel, len(xs), tuple(p[1:] for p in pieces), tuple(depths), total_at, add, tuple(outs), tile),
        out_shape=[pltpu.VMEM((n, width), d) for n, d in shapes],
        in_specs=whole(len(operands)),
        out_specs=whole(len(shapes)),
        input_output_aliases={} if fresh or outs else {len(operands) - 1: 0},
        scratch_shapes=[
            pltpu.VMEM((rows, width), BF16),
            pltpu.VMEM((2 * hidden, width), BF16),
            pltpu.VMEM((hidden, width), BF16),
        ],
        compiler_params=params(limit),
        cost_estimate=pl.CostEstimate(
            flops=rows * width * hidden * 6, bytes_accessed=rows * width * 8 + hidden * width * 6, transcendentals=rows * hidden
        ),
        name="networks",
    )(*(near(a) for a in operands))


def per_device(tokens, routes, gate_num, student_gate, student_up, student_down, teacher_gate, teacher_up, teacher_down):
    here = lax.axis_index("expert").astype(jnp.int32).reshape(1)
    routes, gate_num = routes.T, gate_num.T
    width = tokens.shape[1]
    units = student_gate.shape[2]
    block = EXPERTS * CAP
    half = block // 2
    mib = 1024 * 1024
    cut = units - 128

    student, rows = pack((student_gate[0], student_up[0], student_down[0]), routes, tokens)
    (teacher,) = pack((teacher_gate[0], teacher_up[0], teacher_down[0]))
    prev_student = send(student, ring(1, True))
    next_teacher = send(teacher, ring(-1, True))
    rows, teacher = barrier(rows, teacher)
    rows = rows.reshape(EXPERTS, CAP, width)
    rows = lax.all_to_all(rows, "expert", split_axis=0, concat_axis=0, tiled=True).reshape(block, width)

    prev_rows = send(rows, ring(1, False))
    next_rows = send(rows, ring(-1, False))
    first = [(student, False, 0, units), (teacher, True, 0, units), (prev_student, False, 0, units), (next_teacher, True, 0, units)]
    (total,) = net([rows], first, [512, 768], block, 28 * mib, 4 * block, 3 * block, False)

    parts = split(cut, barrier(student, total)[0], teacher)
    total, prev_student, next_teacher = barrier(total, prev_student, next_teacher)
    far_student = send(prev_student, ring(1, True))
    far_teacher = send(next_teacher, ring(-1, True))
    total, prev_rows, next_rows, *parts = barrier(total, prev_rows, next_rows, *parts)
    far_a = send(prev_rows[:half], ring(1, False))
    far_b = send(next_rows[half:], ring(-1, False))
    first = [(student, False, 0, units), (teacher, True, 0, units), (prev_student, False, 0, units), (next_teacher, True, 0, units)]
    near_xs = [next_rows, prev_rows]
    (total,) = net(near_xs, first, [512, 768], 2 * block, 32 * mib, total, block, False)

    total, *parts = barrier(total, *parts)
    student_a, student_b, teacher_a, teacher_b = parts
    prev_teacher_a = send(teacher_a, ring(1, True))
    next_student_a = send(student_a, ring(-1, True))
    far_xs = [far_a, far_b]
    (total,) = net(far_xs, first, [512, 768], block, 28 * mib, total, 0, False)
    high, low = shares(routes, gate_num)

    total, far_student, far_teacher, student_b, teacher_b = barrier(total, far_student, far_teacher, student_b, teacher_b)
    room = 512 - units
    second = [(far_student, False, 0, units), (far_teacher, True, 0, room)]
    third = [(far_teacher, True, room, units - room), (prev_teacher_a, True, 0, cut), (next_student_a, False, 0, cut)]
    last = [(send(teacher_b, ring(1, True)), True), (send(student_b, ring(-1, True)), False)]
    (total,) = net(far_xs + near_xs + [rows], second, [512], 2 * block, 24 * mib, total, 0, True)
    (total,) = net(far_xs + near_xs + [rows], third, [512], 2 * block, 24 * mib, total, 0, True)
    far_sum = last_net(far_xs, last, total, 0, BF16)
    total, far_sum = barrier(total, far_sum)
    far_sum = send(far_sum, ring(2, False))
    next_same, next_other, prev_same, prev_other = last_net(near_xs, last, total, block, BF16, here)
    total, _ = barrier(total, next_same)
    prev_part, prev_cross = send(next_same, ring(1, False)), send(next_other, cross(1))
    next_part, next_cross = send(prev_same, ring(-1, False)), send(prev_other, cross(-1))
    own = last_net([rows], last, total, 3 * block, F32)
    keep, give = halves(here, own, far_sum)
    given = send(give, cross(0))
    blocks = sum_rows(here, keep, prev_part, next_part, given, prev_cross, next_cross)
    return combine(here, high, low, [send(blocks[step], along_z(step)) if step else blocks[0] for step in STEPS])


def solution(mesh):
    in_specs = (
        P(("expert", "shard"), None),
        P(("expert", "shard"), None),
        P(("expert", "shard"), None),
        P("expert", None, "shard"),
        P("expert", None, "shard"),
        P("expert", "shard", None),
        P("expert", None, "shard"),
        P("expert", None, "shard"),
        P("expert", "shard", None),
    )
    out_specs = P(("expert", "shard"), None)
    return jax.shard_map(
        per_device, mesh=mesh, in_specs=in_specs, out_specs=out_specs, check_vma=False
    )
```

```python
import functools

import jax
import jax.numpy as jnp
from jax import lax
from jax.experimental import pallas as pl
from jax.experimental.pallas import tpu as pltpu
from jax.sharding import PartitionSpec as P

AXES = ("expert", "shard")
BF16 = jnp.bfloat16
F32 = jnp.float32
CAP = 48
EXPERTS = 8
STEPS = (2, 1, 3, 0)
VMEM_LIMIT = 16 * 1024 * 1024


def dev(z, c, y, x):
    return ((z % 4 * 2 + c % 2) * 4 + y % 4) * 4 + x % 4


COORDS = [(z, c, y, x) for z in range(4) for c in range(2) for y in range(4) for x in range(4)]


def ring(step, weights):
    return [
        (dev(z, c, y, x), dev(z, c, y, x + step) if (c == 0) == weights else dev(z, c, y + step, x))
        for z, c, y, x in COORDS
    ]


def cross(step):
    return [(dev(z, c, y, x), dev(z, 1 - c, y + step, x) if c == 0 else dev(z, 1 - c, y, x + step)) for z, c, y, x in COORDS]


def along_z(step):
    return [(dev(z, c, y, x), dev(z + step, c, y, x)) for z, c, y, x in COORDS]


def send(value, pairs):
    return lax.ppermute(value, AXES, pairs)


def barrier(*values):
    return lax.optimization_barrier(values)


def whole(count, space=pltpu.VMEM):
    return [pl.BlockSpec(memory_space=space)] * count


def params(limit=VMEM_LIMIT):
    return pltpu.CompilerParams(vmem_limit_bytes=limit)


def near(value):
    return pltpu.with_memory_space_constraint(value, pltpu.VMEM)


def places(routes_ref):
    tokens = routes_ref.shape[1]
    first, second = routes_ref[0:1, :], routes_ref[1:2, :]
    expert = lax.broadcasted_iota(jnp.int32, (16, tokens), 0)
    named = ((expert == first).astype(F32) + (expert == second).astype(F32)).astype(BF16)
    before = lax.broadcasted_iota(jnp.int32, (tokens, tokens), 0) < lax.broadcasted_iota(jnp.int32, (tokens, tokens), 1)
    earlier = jnp.dot(named, before.astype(F32).astype(BF16), preferred_element_type=F32)
    found = []
    for ids, extra in ((first, 0), (second, (first == second).astype(jnp.int32))):
        slot = jnp.sum(jnp.where(expert == ids, earlier, 0.0), axis=0, keepdims=True).astype(jnp.int32) + extra
        found.append(ids * CAP + slot)
    return found


def pack_kernel(n_rest, *refs):
    weight_refs, rest, packed_ref = refs[:3], refs[3 : 3 + n_rest], refs[3 + n_rest]
    sems = refs[-1]
    units = weight_refs[0].shape[0]
    ins = [
        pltpu.make_async_copy(ref, packed_ref.at[pl.ds(i * units, units)], sems.at[i]) for i, ref in enumerate(weight_refs)
    ]
    for copy in ins:
        copy.start()
    if rest:
        routes_ref, tokens_ref = rest
        first, second = places(routes_ref)
        slots = lax.broadcasted_iota(jnp.int32, (EXPERTS * CAP, tokens_ref.shape[0]), 0)
        chosen = ((slots == first) | (slots == second)).astype(F32).astype(BF16)
        refs[4 + n_rest][...] = jnp.dot(chosen, tokens_ref[...], preferred_element_type=F32).astype(BF16)
    for copy in ins:
        copy.wait()


def pack(weights, *rest):
    gate, up, down = weights
    units, width = down.shape
    rows = [pltpu.VMEM((EXPERTS * CAP, width), BF16)] if rest else []
    return pl.pallas_call(
        functools.partial(pack_kernel, len(rest)),
        out_shape=[pltpu.VMEM((3 * units, width), BF16)] + rows,
        in_specs=whole(3, pltpu.HBM) + whole(len(rest)),
        out_specs=whole(1 + len(rows)),
        scratch_shapes=[pltpu.SemaphoreType.DMA((3,))],
        compiler_params=params(58 * 1024 * 1024 if rest else VMEM_LIMIT),
        cost_estimate=pl.CostEstimate(flops=100_000_000, bytes_accessed=4_000_000, transcendentals=0),
        name="pack_weights",
    )(gate.T, up.T, down, *rest)


def split_kernel(cut, *refs):
    n = len(refs) // 3
    for i in range(n):
        units = refs[i].shape[0] // 3
        for ref, first, count in ((refs[n + 2 * i], 0, cut), (refs[n + 2 * i + 1], cut, units - cut)):
            for k in range(3):
                ref[k * count : (k + 1) * count] = refs[i][k * units + first : k * units + first + count]


def split(cut, *packed):
    shapes = [pltpu.VMEM((3 * n, p.shape[1]), BF16) for p in packed for n in (cut, p.shape[0] // 3 - cut)]
    return pl.pallas_call(
        functools.partial(split_kernel, cut),
        out_shape=shapes,
        in_specs=whole(len(packed)),
        out_specs=whole(len(shapes)),
        compiler_params=params(),
        cost_estimate=pl.CostEstimate(flops=0, bytes_accessed=6_000_000, transcendentals=0),
        name="split_weights",
    )(*(near(p) for p in packed))


def shares_kernel(routes_ref, gates_ref, high_ref, low_ref):
    first, second = places(routes_ref)
    gates = gates_ref[...].astype(F32)
    share = gates / jnp.sum(gates, axis=0, keepdims=True)
    slots = lax.broadcasted_iota(jnp.int32, (EXPERTS * CAP, routes_ref.shape[1]), 0)
    weight = jnp.where(slots == first, share[0:1], 0.0) + jnp.where(slots == second, share[1:2], 0.0)
    weight = weight.T
    high = weight.astype(BF16)
    high_ref[...] = high
    low_ref[...] = (weight - high.astype(F32)).astype(BF16)


def shares(routes, gates):
    tokens = routes.shape[1]
    return pl.pallas_call(
        shares_kernel,
        out_shape=[jax.ShapeDtypeStruct((tokens, EXPERTS * CAP), BF16)] * 2,
        in_specs=whole(2),
        out_specs=whole(2),
        compiler_params=params(),
        cost_estimate=pl.CostEstimate(flops=10_000_000, bytes_accessed=1_000_000, transcendentals=0),
        name="gate_shares",
    )(routes, gates)


def block_of(place):
    return pl.ds(pl.multiple_of(place * CAP, CAP), CAP)


def halves_kernel(here_ref, own_ref, far_ref, keep_ref, give_ref):
    core = here_ref[0] & 1
    for z in range(EXPERTS // 2):
        to = slice(z * CAP, (z + 1) * CAP)
        at = block_of(2 * z + core)
        keep_ref[to] = own_ref[at, :] + far_ref[at, :].astype(F32)
        at = block_of(2 * z + 1 - core)
        give_ref[to] = (own_ref[at, :] + far_ref[at, :].astype(F32)).astype(BF16)


def halves(here, own, far_part):
    rows, width = own.shape
    return pl.pallas_call(
        halves_kernel,
        out_shape=[pltpu.VMEM((rows // 2, width), F32), pltpu.VMEM((rows // 2, width), BF16)],
        in_specs=whole(1, pltpu.SMEM) + whole(2),
        out_specs=whole(2),
        compiler_params=params(),
        cost_estimate=pl.CostEstimate(flops=1_000_000, bytes_accessed=3_000_000, transcendentals=0),
        name="halve_rows",
    )(here, near(own), near(far_part))


def sum_kernel(here_ref, keep_ref, prev_ref, next_ref, given_ref, prev_other_ref, next_other_ref, *out_refs):
    z = here_ref[0] >> 1
    for step, out_ref in enumerate(out_refs):
        at = block_of((z + step) & 3)
        mine = keep_ref[at, :] + prev_ref[at, :].astype(F32) + next_ref[at, :].astype(F32)
        other = given_ref[at, :].astype(F32) + prev_other_ref[at, :].astype(F32) + next_other_ref[at, :].astype(F32)
        out_ref[:CAP] = mine.astype(BF16)
        out_ref[CAP:] = other.astype(BF16)


def sum_rows(here, *parts):
    steps, width = EXPERTS // 2, parts[0].shape[1]
    return pl.pallas_call(
        sum_kernel,
        out_shape=[pltpu.VMEM((2 * CAP, width), BF16)] * steps,
        in_specs=whole(1, pltpu.SMEM) + whole(len(parts)),
        out_specs=whole(steps),
        compiler_params=params(),
        cost_estimate=pl.CostEstimate(flops=1_000_000, bytes_accessed=4_000_000, transcendentals=0),
        name="sum_rows",
    )(here, *(near(p) for p in parts))


def combine_kernel(here_ref, high_ref, low_ref, *refs):
    *block_refs, out_ref, held = refs
    z, core = here_ref[0] >> 1, here_ref[0] & 1
    for step, ref in zip(STEPS, block_refs):
        chip = 2 * ((z - step) & 3)
        held[block_of(chip + core), :] = ref[:CAP]
        held[block_of(chip + 1 - core), :] = ref[CAP:]
    rows = held[...]
    total = jnp.dot(high_ref[...], rows, preferred_element_type=F32)
    total += jnp.dot(low_ref[...], rows, preferred_element_type=F32)
    out_ref[...] = total.astype(BF16)


def combine(here, high, low, blocks):
    tokens, width = high.shape[0], blocks[0].shape[1]
    return pl.pallas_call(
        combine_kernel,
        out_shape=jax.ShapeDtypeStruct((tokens, width), BF16),
        in_specs=whole(1, pltpu.SMEM) + whole(2 + len(blocks)),
        out_specs=pl.BlockSpec(memory_space=pltpu.VMEM),
        scratch_shapes=[pltpu.VMEM((EXPERTS * CAP, width), BF16)],
        compiler_params=params(),
        cost_estimate=pl.CostEstimate(flops=200_000_000, bytes_accessed=1_000_000, transcendentals=0),
        name="combine_rows",
    )(here, near(high), near(low), *(near(b) for b in blocks))


def net_kernel(n_x, pieces, depths, sum_at, add, outs, tile, *refs):
    x_refs, refs = refs[:n_x], refs[n_x:]
    piece_refs, refs = refs[: len(pieces)], refs[len(pieces) :]
    n_sums = len(refs) - max(len(outs), 1) - 3
    if n_sums:
        acc_ref, refs = refs[0], refs[1:]
    if outs:
        out_refs, refs = refs[: len(outs)], refs[len(outs) :]
    else:
        sum_ref, refs = refs[0], refs[1:]
    x, gate_up, down = refs
    rows, width = x.shape
    starts = [sum(depths[:c]) for c in range(len(depths))]

    at = 0
    for ref in x_refs:
        x[at : at + ref.shape[0], :] = ref[...]
        at += ref.shape[0]

    spans, at = [[] for _ in depths], 0
    for ref, (teacher, first, count) in zip(piece_refs, pieces):
        done = 0
        while done < count:
            chunk = max(c for c in range(len(depths)) if starts[c] <= at)
            n = min(count - done, starts[chunk] + depths[chunk] - at)
            spans[chunk].append((ref, teacher, first + done, at - starts[chunk], n))
            at += n
            done += n
    empty = sum(depths) - at

    for c, depth in enumerate(depths):
        low = 2 * starts[c]
        for ref, teacher, first, at, n in spans[c]:
            units = ref.shape[0] // 3
            for k in range(2):
                gate_up[low + k * depth + at : low + k * depth + at + n, :] = ref[k * units + first : k * units + first + n, :]
            part = ref[2 * units + first : 2 * units + first + n, :]
            down[starts[c] + at : starts[c] + at + n, :] = -part if teacher else part
        if empty and c == len(depths) - 1:
            zeros = jnp.zeros((empty, width), BF16)
            for end in (low + depth, low + 2 * depth):
                gate_up[end - empty : end, :] = zeros
            down[starts[c] + depth - empty : starts[c] + depth, :] = zeros

        @pl.loop(0, rows // tile)
        def _(r, c=c, depth=depth, low=low):
            at = pl.ds(pl.multiple_of(r * tile, tile), tile)
            rows_in = x[at, :]
            turned = (((1,), (1,)), ((), ()))
            gate = lax.dot_general(rows_in, gate_up[low : low + depth], turned, preferred_element_type=F32)
            up = lax.dot_general(rows_in, gate_up[low + depth : low + 2 * depth], turned, preferred_element_type=F32)
            hidden = (gate / (1.0 + jnp.exp(-gate)) * up).astype(BF16)
            term = jnp.dot(hidden, down[starts[c] : starts[c] + depth], preferred_element_type=F32)
            within = pl.ds(pl.multiple_of(sum_at + r * tile, EXPERTS * CAP), tile)
            if not outs and (add or c > 0):
                sum_ref[within, :] += term
            elif not outs:
                sum_ref[within, :] = term
            else:
                term += acc_ref[within, :]
                ends = [sum(n for n, _ in outs[: i + 1]) for i in range(len(outs))]
                for t in range(rows // tile):

                    @pl.when(r == t)
                    def _(t=t):
                        for (n, dtype), end, ref in zip(outs, ends, out_refs):
                            if t * tile < end <= (t + 1) * tile:
                                ref[...] = term[end - n - t * tile : end - t * tile].astype(dtype)


def last_kernel(teacher, sum_at, halved, *refs):
    if halved:
        here_ref, *refs, held = refs
        refs, out_refs = refs[:-4], refs[-4:]
        *refs, sum_ref = refs
    else:
        *refs, sum_ref, out_ref = refs
    x_refs, piece_refs = refs[: -len(teacher)], refs[-len(teacher) :]
    x = x_refs[0][...] if len(x_refs) == 1 else jnp.concatenate([r[...] for r in x_refs], axis=0)
    units = piece_refs[0].shape[0] // 3
    turned = (((1,), (1,)), ((), ()))
    gate = lax.dot_general(x, jnp.concatenate([r[:units] for r in piece_refs], axis=0), turned, preferred_element_type=F32)
    up = lax.dot_general(x, jnp.concatenate([r[units : 2 * units] for r in piece_refs], axis=0), turned, preferred_element_type=F32)
    hidden = (gate / (1.0 + jnp.exp(-gate)) * up).astype(BF16)
    down = jnp.concatenate([-r[2 * units :] if negative else r[2 * units :] for r, negative in zip(piece_refs, teacher)], axis=0)
    total = sum_ref[sum_at : sum_at + x.shape[0], :] + jnp.dot(hidden, down, preferred_element_type=F32)
    if not halved:
        out_ref[...] = total.astype(out_ref.dtype)
        return
    held[...] = total
    for i, out_ref in enumerate(out_refs):
        for z in range(EXPERTS // 2):
            place = EXPERTS * (i // 2) + 2 * z + ((here_ref[0] + i) & 1)
            out_ref[z * CAP : (z + 1) * CAP] = held[block_of(place), :].astype(out_ref.dtype)


def last_net(xs, pieces, total, total_at, dtype, here=None):
    rows, width = sum(a.shape[0] for a in xs), xs[0].shape[1]
    halved = here is not None
    hidden = sum(p.shape[0] // 3 for p, _ in pieces)
    operands = list(xs) + [p for p, _ in pieces] + [total]
    return pl.pallas_call(
        functools.partial(last_kernel, tuple(t for _, t in pieces), total_at, halved),
        out_shape=[pltpu.VMEM((rows // 4, width), dtype)] * 4 if halved else pltpu.VMEM((rows, width), dtype),
        in_specs=(whole(1, pltpu.SMEM) if halved else []) + whole(len(operands)),
        out_specs=whole(4) if halved else whole(1)[0],
        scratch_shapes=[pltpu.VMEM((rows, width), F32)] if halved else [],
        compiler_params=params(),
        cost_estimate=pl.CostEstimate(
            flops=rows * width * hidden * 6, bytes_accessed=rows * width * 8 + hidden * width * 6, transcendentals=rows * hidden
        ),
        name="networks_last",
    )(*([here] if halved else []), *(near(a) for a in operands))


def net(xs, pieces, depths, tile, limit, total, total_at, add, outs=()):
    rows, width = sum(a.shape[0] for a in xs), xs[0].shape[1]
    fresh = isinstance(total, int)
    hidden = sum(depths)
    assert not outs or len(depths) == 1
    operands = list(xs) + [p[0] for p in pieces] + ([] if fresh else [total])
    shapes = outs or [(total if fresh else total.shape[0], F32)]
    return pl.pallas_call(
        functools.partial(net_kernel, len(xs), tuple(p[1:] for p in pieces), tuple(depths), total_at, add, tuple(outs), tile),
        out_shape=[pltpu.VMEM((n, width), d) for n, d in shapes],
        in_specs=whole(len(operands)),
        out_specs=whole(len(shapes)),
        input_output_aliases={} if fresh or outs else {len(operands) - 1: 0},
        scratch_shapes=[
            pltpu.VMEM((rows, width), BF16),
            pltpu.VMEM((2 * hidden, width), BF16),
            pltpu.VMEM((hidden, width), BF16),
        ],
        compiler_params=params(limit),
        cost_estimate=pl.CostEstimate(
            flops=rows * width * hidden * 6, bytes_accessed=rows * width * 8 + hidden * width * 6, transcendentals=rows * hidden
        ),
        name="networks",
    )(*(near(a) for a in operands))


def per_device(tokens, routes, gate_num, student_gate, student_up, student_down, teacher_gate, teacher_up, teacher_down):
    here = lax.axis_index("expert").astype(jnp.int32).reshape(1)
    routes, gate_num = routes.T, gate_num.T
    width = tokens.shape[1]
    units = student_gate.shape[2]
    block = EXPERTS * CAP
    half = block // 2
    mib = 1024 * 1024
    cut = units - 128

    student, rows = pack((student_gate[0], student_up[0], student_down[0]), routes, tokens)
    (teacher,) = pack((teacher_gate[0], teacher_up[0], teacher_down[0]))
    prev_student = send(student, ring(1, True))
    next_teacher = send(teacher, ring(-1, True))
    rows, teacher = barrier(rows, teacher)
    rows = rows.reshape(EXPERTS, CAP, width)
    rows = lax.all_to_all(rows, "expert", split_axis=0, concat_axis=0, tiled=True).reshape(block, width)

    prev_rows = send(rows, ring(1, False))
    next_rows = send(rows, ring(-1, False))
    first = [(student, False, 0, units), (teacher, True, 0, units), (prev_student, False, 0, units), (next_teacher, True, 0, units)]
    (total,) = net([rows], first, [512, 768], block, 28 * mib, 4 * block, 3 * block, False)

    parts = split(cut, barrier(student, total)[0], teacher)
    total, prev_student, next_teacher = barrier(total, prev_student, next_teacher)
    far_student = send(prev_student, ring(1, True))
    far_teacher = send(next_teacher, ring(-1, True))
    total, prev_rows, next_rows, *parts = barrier(total, prev_rows, next_rows, *parts)
    far_a = send(prev_rows[:half], ring(1, False))
    far_b = send(next_rows[half:], ring(-1, False))
    first = [(student, False, 0, units), (teacher, True, 0, units), (prev_student, False, 0, units), (next_teacher, True, 0, units)]
    near_xs = [next_rows, prev_rows]
    (total,) = net(near_xs, first, [512, 768], 2 * block, 32 * mib, total, block, False)

    total, *parts = barrier(total, *parts)
    student_a, student_b, teacher_a, teacher_b = parts
    prev_teacher_a = send(teacher_a, ring(1, True))
    next_student_a = send(student_a, ring(-1, True))
    far_xs = [far_a, far_b]
    (total,) = net(far_xs, first, [512, 768], block, 28 * mib, total, 0, False)
    high, low = shares(routes, gate_num)

    total, far_student, far_teacher, student_b, teacher_b = barrier(total, far_student, far_teacher, student_b, teacher_b)
    room = 512 - units
    second = [(far_student, False, 0, units), (far_teacher, True, 0, room)]
    third = [(far_teacher, True, room, units - room), (prev_teacher_a, True, 0, cut), (next_student_a, False, 0, cut)]
    last = [(send(teacher_b, ring(1, True)), True), (send(student_b, ring(-1, True)), False)]
    (total,) = net(far_xs + near_xs + [rows], second, [512], 2 * block, 24 * mib, total, 0, True)
    (total,) = net(far_xs + near_xs + [rows], third, [512], 2 * block, 24 * mib, total, 0, True)
    far_sum = last_net(far_xs, last, total, 0, BF16)
    total, far_sum = barrier(total, far_sum)
    far_sum = send(far_sum, ring(2, False))
    next_same, next_other, prev_same, prev_other = last_net(near_xs, last, total, block, BF16, here)
    total, _ = barrier(total, next_same)
    prev_part, prev_cross = send(next_same, ring(1, False)), send(next_other, cross(1))
    next_part, next_cross = send(prev_same, ring(-1, False)), send(prev_other, cross(-1))
    own = last_net([rows], last, total, 3 * block, F32)
    keep, give = halves(here, own, far_sum)
    given = send(give, cross(0))
    blocks = sum_rows(here, keep, prev_part, next_part, given, prev_cross, next_cross)
    return combine(here, high, low, [send(blocks[step], along_z(step)) if step else blocks[0] for step in STEPS])


def solution(mesh):
    in_specs = (
        P(("expert", "shard"), None),
        P(("expert", "shard"), None),
        P(("expert", "shard"), None),
        P("expert", None, "shard"),
        P("expert", None, "shard"),
        P("expert", "shard", None),
        P("expert", None, "shard"),
        P("expert", None, "shard"),
        P("expert", "shard", None),
    )
    out_specs = P(("expert", "shard"), None)
    return jax.shard_map(
        per_device, mesh=mesh, in_specs=in_specs, out_specs=out_specs, check_vma=False
    )
```
